256 devices in a mesh: tok: 8 (over z), proto: 32 (over x, y, core).
Axes of the slice: x: 4, y: 4, z: 8, core: 2. Of those that a mesh axis runs over, the one named last changes fastest.
Arguments:
- teacher_hidden: bfloat16 [16384, 2048], P('tok'), may hold values from -6 to 6
- head_teacher: bfloat16 [2048, 256], P('proto'), may hold values from -0.125 to 0.125
- proto_teacher: bfloat16 [256, 65536], P('tok', 'proto'), may hold values from -1.25 to 1.25
- student_hidden: bfloat16 [2048, 2048], P('tok'), may hold values from -0.0625 to 0.8
- head_student: bfloat16 [2048, 256], P('proto'), may hold values from -0.0625 to 0.0625
- proto_student: bfloat16 [256, 65536], P('tok', 'proto'), may hold values from -0.25 to 0.25
- mask_index: int32 [2048], P('tok'), may hold values from 0 to 2047
- mask_count: int32 [8], replicated, may hold values from 32 to 256, as said below
Outputs:
- row_loss: float32 [2048], P('tok')
- hidden_grad: bfloat16 [2048, 2048], P('tok')
The draws below stay inside these ranges and needn't reach their ends.
Inputs may be any that keep to these rules, and one draw needn't show every extreme that they name: `mask_index`: a row among the teacher tokens held by the same index of tok. `mask_count`: in every draw one index of tok has all 256 slots live.
All inputs are finite; a program needn't handle non-finite values.
Results may differ from the reference program's by a relative error of at most 0.0056.
Values may be sent and summed in bfloat16 or wider, within the bound.
No kernel may reach another device: no remote copies, remote signals or barrier semaphores. Data moves between devices by JAX's collectives and lax.ppermute only.
A program may use at most 128 MiB of HBM per device.

```python
import math
import jax
import jax.numpy as jnp
from jax import lax

H = 2048
D = 256
PROTOS = 65536
TOK_DEV = 2048
M_DEV = 256
ITERS = 3
TOKENS = 16384
MASKED = 2048
GROUPS = 8


def draw_mask_count(key, part):
    key = jax.random.fold_in(key, 11)
    counts = jax.random.randint(key, (GROUPS,), M_DEV // 8, M_DEV // 2 + 1)
    busiest = jax.random.randint(jax.random.fold_in(key, 1), (), 0, GROUPS)
    return jnp.where(jnp.arange(GROUPS) == busiest, M_DEV, counts).astype(jnp.int32)


def draw_teacher_hidden(key, part):
    key = jax.random.fold_in(key, 31)
    signs = jnp.where(jax.random.bernoulli(jax.random.fold_in(key, 1), 0.5, (1, H)), 1.0, -1.0)
    noise = jax.random.truncated_normal(jax.random.fold_in(key, 2), -3.5, 3.5, (TOKENS, H), jnp.float32)
    amplitude = jax.random.uniform(jax.random.fold_in(key, 4), (TOKENS, 1), jnp.float32, 0.0, 2.0)
    return (noise + amplitude * signs).astype(jnp.bfloat16)


def shared_head(key):
    return 0.02 * jax.random.truncated_normal(key, -3.0, 3.0, (H, D), jnp.float32)


def draw_head_student(key, part):
    head_matrix = shared_head(key)
    return head_matrix.astype(jnp.bfloat16)


def draw_proto_student(key, part):
    head_matrix = shared_head(key)
    key = jax.random.fold_in(key, 23)
    unit_ids = jax.random.randint(jax.random.fold_in(key, 1), (PROTOS,), 0, H)
    weights = jax.random.uniform(jax.random.fold_in(key, 2), (1, PROTOS), jnp.float32, 1.0, 3.0)
    jitter = 0.02 * jax.random.truncated_normal(jax.random.fold_in(key, 3), -3.0, 3.0, (D, PROTOS), jnp.float32)
    aligned = jnp.transpose(jnp.take(head_matrix, unit_ids, axis=0)) * weights
    return (aligned + jitter).astype(jnp.bfloat16)


def draw_student_hidden(key, part):
    key = jax.random.fold_in(key, 29)
    noise_scale = 0.12 / math.sqrt(H)
    unit_ids = jax.random.randint(jax.random.fold_in(key, 1), (MASKED, 1), 0, H)
    heights = jax.random.uniform(jax.random.fold_in(key, 2), (MASKED, 1), jnp.float32, 0.144, 0.36)
    spikes = jnp.where(jnp.arange(H, dtype=jnp.int32)[None, :] == unit_ids, heights, 0.0)
    jitter = jax.random.truncated_normal(jax.random.fold_in(key, 3), -4.0, 4.0, (MASKED, H), jnp.float32)
    return (noise_scale * jitter + spikes).astype(jnp.bfloat16)


def with_ends(entries, own_key, least, high):
    place = [jax.random.randint(jax.random.fold_in(own_key, axis), (), 0, length) for axis, length in enumerate(entries.shape)]
    widest = entries.shape.index(max(entries.shape))
    beside = place[:widest] + [(place[widest] + 1) % entries.shape[widest]] + place[widest + 1:]
    return entries.at[tuple(place)].set(least).at[tuple(beside)].set(high)


def block_scale(key, dims, pieces, smallest, high):
    def one(dim, blocks):
        steps = jax.random.uniform(jax.random.fold_in(jax.random.fold_in(key, 6), dim), (blocks,), jnp.float32, smallest / len(pieces), high / len(pieces))
        return jnp.repeat(jnp.exp(steps), dims[dim] // blocks).reshape((-1,) + (1,) * (len(dims) - dim - 1))

    factor_of = one(*pieces[0])
    for cut in pieces[1:]:
        factor_of = factor_of * one(*cut)
    return factor_of


def bell_draw(key, dims, deviation, limit, pieces=(), held_as=jnp.bfloat16):
    values = jax.random.normal(key, dims, jnp.float32) * deviation
    if len(pieces) > 0:
        values = block_scale(key, dims, pieces, -0.22, 0.18) * values
    return jnp.clip(values, min=-limit, max=limit).astype(held_as)


def setup_inputs(seed: int = 0) -> dict:
    streams_of = jax.random.split(jax.random.key(seed), 9)
    return {
        "teacher_hidden": draw_teacher_hidden(jax.random.fold_in(streams_of[8], 71), 0),
        "head_teacher": bell_draw(streams_of[1], (H, D), H ** -0.5, 0.125, ((0, 32),)),
        "proto_teacher": bell_draw(streams_of[2], (D, PROTOS), 24 ** -0.5, 1.25, ((0, 8), (1, 32))),
        "student_hidden": draw_student_hidden(jax.random.fold_in(streams_of[8], 71), 0),
        "head_student": draw_head_student(jax.random.fold_in(streams_of[8], 71), 0),
        "proto_student": draw_proto_student(jax.random.fold_in(streams_of[8], 71), 0),
        "mask_index": with_ends(jax.random.randint(streams_of[6], (MASKED,), 0, TOK_DEV), jax.random.fold_in(streams_of[6], 1), 0, TOK_DEV - 1).astype(jnp.int32),
        "mask_count": draw_mask_count(jax.random.fold_in(streams_of[8], 71), 0),
    }


teacher_temp = 0.07
student_temp = 0.1
norm_eps = 1e-06

def unit_rows(values):
    scale = lax.rsqrt(lax.optimization_barrier(jnp.sum(values * values, axis=1, keepdims=True)) + norm_eps)
    return (values * scale, scale)

def reference(teacher_hidden, head_teacher, proto_teacher, student_hidden, head_student, proto_student, mask_index, mask_count):
    teacher_neck = jnp.dot(teacher_hidden, head_teacher, preferred_element_type=jnp.float32)
    unit_teacher = unit_rows(teacher_neck)[0].astype(jnp.bfloat16)
    assign = jnp.exp(jnp.dot(unit_teacher, proto_teacher, preferred_element_type=jnp.float32) / teacher_temp)
    for sweep in range(ITERS):
        proto_sums = lax.optimization_barrier(jnp.sum(assign, axis=0, keepdims=True))
        assign = assign / (PROTOS * proto_sums)
        token_sums = lax.optimization_barrier(jnp.sum(assign, axis=1, keepdims=True))
        assign = assign / (TOKENS * token_sums)
    slot_ids = jnp.arange(MASKED, dtype=jnp.int32)
    groups = (slot_ids // M_DEV).astype(jnp.int32)
    picked_rows = (groups * TOK_DEV + mask_index).astype(jnp.int32)
    targets = jnp.take(assign, picked_rows, axis=0) * TOKENS
    live_rows = (slot_ids % M_DEV < jnp.take(mask_count, groups)).astype(jnp.float32)
    student_neck = jnp.dot(student_hidden, head_student, preferred_element_type=jnp.float32)
    unit_float, feat_scale = unit_rows(student_neck)
    unit_student = unit_float.astype(jnp.bfloat16)
    proto_scale = lax.rsqrt(lax.optimization_barrier(jnp.sum(jnp.square(proto_student.astype(jnp.float32)), axis=0)) + norm_eps)
    logits = jnp.dot(unit_student, proto_student, preferred_element_type=jnp.float32) * proto_scale / student_temp
    exp_logits = jnp.exp(logits)
    totals = lax.optimization_barrier(jnp.sum(exp_logits, axis=1))
    target_dot = lax.optimization_barrier(jnp.sum(targets * logits, axis=1))
    row_loss = live_rows * (jnp.log(totals) - target_dot)
    logit_grad = (live_rows[:, None] * (exp_logits / totals[:, None] - targets) * proto_scale / student_temp).astype(jnp.bfloat16)
    unit_grad = jnp.dot(logit_grad, proto_student.T, preferred_element_type=jnp.float32)
    inner = lax.optimization_barrier(jnp.sum(unit_float * unit_grad, axis=1, keepdims=True))
    neck_grad = (feat_scale * (unit_grad - unit_float * inner)).astype(jnp.bfloat16)
    hidden_grad = jnp.dot(neck_grad, head_student.T, preferred_element_type=jnp.float32).astype(jnp.bfloat16)
    return (row_loss, hidden_grad)
```

```python
import jax
import jax.numpy as jnp
from jax import lax
from jax.sharding import PartitionSpec as P

teacher_temp = 0.07
student_temp = 0.1
norm_eps = 1e-06
LOG2E = 1.4426950408889634
f32 = jnp.float32
bf16 = jnp.bfloat16


def unit_rows(values):
    scale = lax.rsqrt(jnp.sum(values * values, axis=1, keepdims=True) + norm_eps)
    return (values * scale, scale)


def exchange(blocks, axis, groups=None):
    return lax.all_to_all(blocks, axis, 0, 0, tiled=True, axis_index_groups=groups)


def copies(values, count):
    return jnp.broadcast_to(values[None], (count,) + values.shape)


def total(values, axis, count):
    return jnp.sum(exchange(copies(values, count), axis), axis=0)


def gather_heads(block, count):
    chips = count // 2
    groups = [[2 * k + c for k in range(chips)] for c in range(2)]
    mine = exchange(copies(block, chips), "proto", groups)
    other = lax.ppermute(mine, "proto", [(i, i ^ 1) for i in range(count)])
    first = lax.axis_index("proto") % 2 == 0
    both = jnp.stack([jnp.where(first, mine, other), jnp.where(first, other, mine)], axis=1)
    return both.reshape(count * block.shape[0], block.shape[1])


def split_dot(left, right):
    high = left.astype(bf16)
    low = (left - high.astype(f32)).astype(bf16)
    dims = (((1,), (1,)), ((), ()))
    return lax.dot_general(high, right, dims, preferred_element_type=f32) + lax.dot_general(
        low, right, dims, preferred_element_type=f32
    )


def shards(
    teacher_hidden,
    head_teacher,
    proto_teacher,
    student_hidden,
    head_student,
    proto_student,
    mask_index,
    mask_count,
):
    toks = lax.axis_size("tok")
    protos = lax.axis_size("proto")
    tok_dev = teacher_hidden.shape[0]
    slot_dev = student_hidden.shape[0]
    width = head_teacher.shape[1]
    whole_teacher = lax.all_gather(proto_teacher, "tok", axis=0, tiled=True)
    heads = gather_heads(jnp.concatenate([head_teacher, head_student], axis=1), protos)
    teacher_neck = jnp.dot(teacher_hidden, heads[:, :width], preferred_element_type=f32)
    unit_teacher = unit_rows(teacher_neck)[0].astype(bf16)
    student_neck = jnp.dot(student_hidden, heads[:, width:], preferred_element_type=f32)
    unit_float, feat_scale = unit_rows(student_neck)
    unit_student = unit_float.astype(bf16)
    chosen = (mask_index[:, None] == jnp.arange(tok_dev, dtype=jnp.int32)[None, :]).astype(bf16)
    unit_masked = jnp.dot(chosen, unit_teacher, preferred_element_type=f32).astype(bf16)

    whole_student = lax.all_gather(
        lax.optimization_barrier((proto_student, whole_teacher))[0], "tok", axis=0, tiled=True
    )

    fold = LOG2E / teacher_temp
    scores = jnp.exp2(jnp.dot(unit_teacher, whole_teacher, preferred_element_type=f32) * fold)
    masked = jnp.exp2(jnp.dot(unit_masked, whole_teacher, preferred_element_type=f32) * fold)
    column = jnp.sum(scores, axis=0)
    scores = scores.astype(bf16)
    for sweep in range(2):
        inverse = 1.0 / total(column, "tok", toks)
        row = jnp.sum(scores.astype(f32) * inverse[None, :], axis=1)
        weight = 1.0 / total(row, "proto", protos)
        column = jnp.sum(scores.astype(f32) * weight[:, None], axis=0)
    inverse = 1.0 / total(column, "tok", toks)

    proto_scale = lax.rsqrt(
        jnp.sum(jnp.square(whole_student.astype(f32)), axis=0) + norm_eps
    ) / student_temp
    logits = jnp.dot(unit_student, whole_student, preferred_element_type=f32) * proto_scale
    exp_logits = jnp.exp(logits)
    grad_soft = split_dot(exp_logits * proto_scale, whole_student)
    goal = masked * inverse[None, :]
    grad_goal = split_dot(goal * proto_scale, whole_student)
    stats = jnp.stack(
        [jnp.sum(exp_logits, axis=1), jnp.sum(goal, axis=1), jnp.sum(goal * logits, axis=1)], axis=1
    )
    stats = jnp.pad(stats, ((0, 0), (0, 125)))
    parts = jnp.concatenate([grad_soft, grad_goal, stats], axis=1)
    share = slot_dev // protos
    parts = parts.reshape(protos, share, 2 * width + 128)
    mine = jnp.sum(exchange(parts, "proto"), axis=0)
    soft_total = mine[:, 2 * width : 2 * width + 1]
    goal_total = mine[:, 2 * width + 1 : 2 * width + 2]
    goal_dot = mine[:, 2 * width + 2 : 2 * width + 3]
    first = lax.axis_index("proto") * share
    slot_ids = first + jnp.arange(share, dtype=jnp.int32)
    live = (slot_ids < jnp.take(mask_count, lax.axis_index("tok"))).astype(f32)[:, None]
    loss = live * (jnp.log(soft_total) - goal_dot / goal_total)
    unit_grad = live * (mine[:, :width] / soft_total - mine[:, width : 2 * width] / goal_total)
    my_unit = lax.dynamic_slice_in_dim(unit_float, first, share, 0)
    my_scale = lax.dynamic_slice_in_dim(feat_scale, first, share, 0)
    inner = jnp.sum(my_unit * unit_grad, axis=1, keepdims=True)
    neck_grad = (my_scale * (unit_grad - my_unit * inner)).astype(bf16)
    top = loss.astype(bf16)
    rest = loss - top.astype(f32)
    mid = rest.astype(bf16)
    low = (rest - mid.astype(f32)).astype(bf16)
    final = jnp.concatenate(
        [neck_grad, top, mid, low, jnp.zeros((share, 125), bf16)], axis=1
    )
    final = exchange(copies(final, protos), "proto").reshape(slot_dev, width + 128)
    tail = final[:, width : width + 3].astype(f32)
    row_loss = tail[:, 0] + tail[:, 1] + tail[:, 2]
    hidden_grad = lax.dot_general(
        final[:, :width], heads[:, width:], (((1,), (1,)), ((), ())), preferred_element_type=f32
    ).astype(bf16)
    return (row_loss, hidden_grad)


def solution(mesh):
    placed = (
        P("tok", None),
        P("proto", None),
        P("tok", "proto"),
        P("tok", None),
        P("proto", None),
        P("tok", "proto"),
        P("tok"),
        P(),
    )
    return jax.shard_map(
        shards, mesh=mesh, in_specs=placed, out_specs=(P("tok"), P("tok", None)), check_vma=False
    )
```

```python
import jax
import jax.numpy as jnp
from jax import lax
from jax.experimental import pallas as pl
from jax.experimental.pallas import tpu as pltpu
from jax.sharding import PartitionSpec as P

teacher_temp = 0.07
student_temp = 0.1
norm_eps = 1e-06
LOG2E = 1.4426950408889634
MIB = 1024 * 1024
f32 = jnp.float32
bf16 = jnp.bfloat16
VM = pl.BlockSpec(memory_space=pltpu.VMEM)
SM = pl.BlockSpec(memory_space=pltpu.SMEM)
HB = pl.BlockSpec(memory_space=pltpu.HBM)
ANY = pl.BlockSpec(memory_space=pl.ANY)
NT = (((1,), (1,)), ((), ()))


def shaped(shape, dtype):
    return jax.ShapeDtypeStruct(shape, dtype)


def call(kernel, out_shape, in_specs, out_specs, cost, scratch=(), mib=40):
    return pl.pallas_call(
        kernel,
        out_shape=out_shape,
        in_specs=in_specs,
        out_specs=out_specs,
        scratch_shapes=list(scratch),
        cost_estimate=pl.CostEstimate(flops=cost[0], bytes_accessed=cost[1], transcendentals=0),
        compiler_params=pltpu.CompilerParams(vmem_limit_bytes=mib * MIB),
    )


def held(values):
    return pltpu.with_memory_space_constraint(values, pltpu.VMEM)


def dot(left, right, dims=(((1,), (0,)), ((), ()))):
    return lax.dot_general(left, right, dims, preferred_element_type=f32)


def split(values):
    high = values.astype(bf16)
    return high, (values - high.astype(f32)).astype(bf16)


def fetch(pairs, sems, first=0):
    copies = [
        pltpu.make_async_copy(source, target, sems.at[first + k])
        for k, (source, target) in enumerate(pairs)
    ]
    for copy in copies:
        copy.start()
    return copies


def settle(copies):
    for copy in copies:
        copy.wait()


def heads_kernel(teacher, student, first, second, copies, both, v_teacher, v_student, sems):
    rows, width = first.shape[0], teacher.shape[1]
    heads = fetch([(teacher, v_teacher), (student, v_student)], sems)
    rest = fetch(
        [(first, both.at[pl.ds(0, rows), :]), (second, both.at[pl.ds(rows, rows), :])], sems, 2
    )
    settle(heads)
    copies[:, :, :width] = jnp.broadcast_to(v_teacher[...][None], copies.shape[:2] + (width,))
    copies[:, :, width:] = jnp.broadcast_to(v_student[...][None], copies.shape[:2] + (width,))
    settle(rest)


def neck_kernel(core, hidden, mine, other, unit, kept, student, head, tokens, sems):
    chips, rows, double = mine.shape
    width = double // 2
    near, far = core[0] * rows, (1 - core[0]) * rows
    near, far = (pl.ds(pl.multiple_of(at, rows), rows) for at in (near, far))
    heads = fetch(
        [
            (mine.at[:, :, :width], head.at[:, near, :]),
            (other.at[:, :, :width], head.at[:, far, :]),
        ],
        sems,
    )
    count = tokens.shape[0]
    step = tokens.shape[1]
    blocks = fetch(
        [(hidden.at[pl.ds(k * step, step), :], tokens.at[k]) for k in range(count)], sems, 2
    )
    rest = fetch(
        [
            (mine.at[:, :, width:], student.at[:, near, :]),
            (other.at[:, :, width:], student.at[:, far, :]),
        ],
        sems,
        2 + count,
    )
    settle(heads)
    weights = head[...].reshape(chips * 2 * rows, width)
    for k in range(count):
        blocks[k].wait()
        neck = dot(tokens[k], weights)
        scale = lax.rsqrt(jnp.sum(neck * neck, axis=1, keepdims=True) + norm_eps)
        unit[k * step : (k + 1) * step, :] = (neck * scale).astype(bf16)
    settle(rest + fetch([(unit, kept)], sems, 4 + count))


def ring_pairs(tok, blocks, whole, which):
    rows = blocks[0].shape[0] // 2
    count = whole.shape[0] // rows
    pairs = []
    for k, block in enumerate(blocks):
        hop = (k + 1) // 2
        if 2 * hop < count:
            part = block.at[pl.ds(which * rows, rows), :]
        elif k % 2 != which:
            part = block
        else:
            continue
        origin = lax.rem(tok + (count - hop if k % 2 == 1 else hop), count) * rows
        pairs.append((part, whole.at[pl.ds(pl.multiple_of(origin, rows), rows), :]))
    return pairs


def scores_kernel(tok, unit, *refs):
    blocks, refs = refs[:-7], refs[-7:]
    scores, teacher, student, columns, whole, sums, sems = refs
    copies = fetch(ring_pairs(tok[0], blocks, whole, 0), sems)
    rest = fetch(ring_pairs(tok[0], blocks, student, 1), sems, len(copies))
    settle(copies)
    rest = rest + fetch([(whole, teacher)], sems, len(copies + rest))
    fold = LOG2E / teacher_temp
    step = 256
    count = step // 128

    def over_columns(c, _):
        at = pl.ds(pl.multiple_of(c * step, step), step)
        weights = whole[:, at]
        acc = jnp.zeros((8, step), f32)
        for r in range(unit.shape[0] // step):
            rows = slice(r * step, (r + 1) * step)
            value = jnp.exp2(dot(unit[rows, :], weights) * fold)
            scores[rows, at] = value.astype(bf16)
            acc = acc + jnp.sum(value.reshape(step // 8, 8, step), axis=0)
        acc = jnp.sum(acc, axis=0, keepdims=True)
        for k in range(count):
            sums[pl.ds(c * count + k, 1), :] = acc[:, k * 128 : (k + 1) * 128]
        return 0

    lax.fori_loop(0, whole.shape[1] // step, over_columns, 0)
    settle(rest)
    columns[...] = jnp.broadcast_to(sums[...][None], columns.shape)


def row_kernel(parts, scores, rows, sums):
    inverse = 1.0 / jnp.sum(parts[...], axis=0)
    group = 4

    def over_rows(i, _):
        for r in range(group):
            at = pl.ds(pl.multiple_of(i * (group * 128) + r * 128, 128), 128)
            acc = jnp.zeros((128, 128), f32)
            for c in range(scores.shape[1] // 128):
                block = scores[at, c * 128 : (c + 1) * 128].astype(f32)
                acc = acc + block * inverse[c : c + 1, :]
            sums[pl.ds(i * group + r, 1), :] = jnp.sum(acc.T, axis=0, keepdims=True)
        return 0

    lax.fori_loop(0, scores.shape[0] // (group * 128), over_rows, 0)
    rows[...] = jnp.broadcast_to(sums[...][None], rows.shape)


def column_kernel(parts, scores, columns, weight):
    turned = (1.0 / jnp.sum(parts[...], axis=0)).T
    for r in range(weight.shape[0] // 128):
        weight[r * 128 : (r + 1) * 128, :] = jnp.broadcast_to(turned[:, r : r + 1], (128, 128))
    step = 64
    tiles = scores.shape[1] // 128

    def over_rows(r, acc):
        at = pl.ds(pl.multiple_of(r * step, step), step)
        w = weight[at, :]
        out = []
        for c in range(tiles):
            block = scores[at, c * 128 : (c + 1) * 128].astype(f32) * w
            out.append(acc[c] + jnp.sum(block.reshape(step // 8, 8, 128), axis=0))
        return tuple(out)

    zeros = tuple(jnp.zeros((8, 128), f32) for _ in range(tiles))
    acc = lax.fori_loop(0, scores.shape[0] // step, over_rows, zeros, unroll=4)
    total = jnp.concatenate([jnp.sum(a, axis=0, keepdims=True) for a in acc], axis=0)
    columns[...] = jnp.broadcast_to(total[None], columns.shape)


def student_kernel(index, hidden, head, unit, teacher, student, *refs):
    masked, scale_out, unit_out, norm, grad, total = refs[:6]
    v_hidden, v_head, v_unit, v_teacher, whole, sems = refs[6:]
    copies = fetch(
        [
            (hidden, v_hidden),
            (head, v_head),
            (unit, v_unit),
            (teacher, v_teacher),
            (student, whole),
        ],
        sems,
    )
    slots, tokens = v_hidden.shape[0], v_unit.shape[0]
    settle(copies[:2])
    neck = dot(v_hidden[...], v_head[...])
    scale = lax.rsqrt(jnp.sum(neck * neck, axis=1, keepdims=True) + norm_eps)
    unit_float = neck * scale
    unit_out[...] = unit_float
    norm[...] = jnp.broadcast_to(scale, norm.shape)
    student = unit_float.astype(bf16)
    settle(copies[2:])
    wanted = jnp.broadcast_to(index[...].astype(f32), (128, slots)).T[:, 0:1]
    chosen = wanted == lax.broadcasted_iota(jnp.int32, (slots, tokens), 1).astype(f32)
    picked = dot(chosen.astype(f32).astype(bf16), v_unit[...]).astype(bf16)
    fold = LOG2E / teacher_temp
    step = 256
    grad_acc = jnp.zeros(grad.shape, f32)
    total_acc = jnp.zeros((slots, 1), f32)
    for c in range(whole.shape[1] // step):
        at = slice(c * step, (c + 1) * step)
        masked[:, at] = jnp.exp2(dot(picked, v_teacher[:, at]) * fold)
        weights = whole[:, at]
        wide = weights.astype(f32)
        scale_p = lax.rsqrt(jnp.sum(wide * wide, axis=0, keepdims=True) + norm_eps) / student_temp
        scale_out[:, at] = jnp.broadcast_to(scale_p, (8, step))
        soft = jnp.exp2(dot(student, weights) * (scale_p * LOG2E))
        total_acc = total_acc + jnp.sum(soft, axis=1, keepdims=True)
        high, low = split(soft * scale_p)
        grad_acc = grad_acc + dot(high, weights, NT) + dot(low, weights, NT)
    grad[...] = grad_acc
    total[...] = jnp.broadcast_to(total_acc, total.shape)


def goal_kernel(
    parts, masked, scale_p, whole, grad, total, out, v_masked, v_scale, v_whole, v_total, sems
):
    slots, width = grad.shape
    step = 512
    count = whole.shape[1] // step
    copies = fetch([(scale_p, v_scale), (total, v_total), (grad, out.at[:, :width])], sems)
    blocks = []
    for c in range(count):
        at = pl.ds(c * step, step)
        blocks.append(
            fetch(
                [(masked.at[:, at], v_masked.at[:, at]), (whole.at[:, at], v_whole.at[:, at])],
                sems,
                3 + 2 * c,
            )
        )
    inverse = 1.0 / jnp.sum(parts[...], axis=0)
    grad_acc = jnp.zeros((slots, width), f32)
    goal_acc = jnp.zeros((slots, 128), f32)
    settle(copies[:1])
    for c in range(count):
        settle(blocks[c])
        pieces = []
        for k in range(c * (step // 128), (c + 1) * (step // 128)):
            at = slice(k * 128, (k + 1) * 128)
            goal = v_masked[:, at] * inverse[k : k + 1, :]
            goal_acc = goal_acc + goal
            pieces.append(goal * v_scale[0:1, at])
        high, low = split(jnp.concatenate(pieces, axis=1))
        weights = v_whole[:, c * step : (c + 1) * step]
        grad_acc = grad_acc + dot(high, weights, NT) + dot(low, weights, NT)
    out[:, width : 2 * width] = grad_acc
    goal_total = jnp.sum(goal_acc, axis=1, keepdims=True)
    lane = lax.broadcasted_iota(jnp.int32, (slots, 128), 1)
    settle(copies[1:])
    out[:, 2 * width :] = jnp.where(lane == 0, v_total[...], goal_total)


def slots_kernel(place, parts, unit_float, norm, out, v_unit, v_norm, sems):
    share, width = parts.shape[1], unit_float.shape[1]
    at = pl.multiple_of(place[0] * share, share)
    copies = fetch(
        [(unit_float.at[pl.ds(at, share), :], v_unit), (norm.at[pl.ds(at, share), :], v_norm)], sems
    )
    mine = jnp.sum(parts[...], axis=0)
    settle(copies)
    unit = v_unit[...]
    scale = v_norm[:, 0:1]
    soft_total = mine[:, 2 * width : 2 * width + 1]
    goal_total = mine[:, 2 * width + 1 : 2 * width + 2]
    soft, goal = mine[:, :width] / soft_total, mine[:, width : 2 * width] / goal_total
    slot = at + lax.broadcasted_iota(jnp.int32, (share, 1), 0)
    live = jnp.where(slot < place[1], 1.0, 0.0)
    target_dot = jnp.sum(unit.astype(bf16).astype(f32) * goal, axis=1, keepdims=True)
    loss = live * (jnp.log(soft_total) - target_dot)
    unit_grad = live * (soft - goal)
    inner = jnp.sum(unit * unit_grad, axis=1, keepdims=True)
    neck_grad = scale * (unit_grad - unit * inner)
    top = loss.astype(bf16).astype(f32)
    mid = (loss - top).astype(bf16).astype(f32)
    low = loss - top - mid
    lane = lax.broadcasted_iota(jnp.int32, (share, width), 1)
    tail = jnp.where(lane == 0, top, jnp.where(lane == 1, mid, jnp.where(lane == 2, low, 0.0)))
    both = jnp.concatenate([neck_grad, tail], axis=0).astype(bf16)
    out[...] = jnp.broadcast_to(both[None], out.shape)


def hidden_kernel(parts, head, hidden, loss):
    count, double, width = parts.shape
    share = double // 2
    wide = parts[...].astype(f32)
    neck_grad = wide[:, :share, :].reshape(count * share, width).astype(bf16)
    tail = wide[:, share:, :128].reshape(count * share, 128).T
    loss[...] = tail[0:1, :] + tail[1:2, :] + tail[2:3, :]
    step = 512
    for c in range(head.shape[0] // step):
        at = slice(c * step, (c + 1) * step)
        hidden[:, at] = dot(neck_grad, head[at, :], NT).astype(bf16)


def exchange(blocks, axis, groups=None):
    return lax.all_to_all(blocks, axis, 0, 0, tiled=True, axis_index_groups=groups)


def shards(
    teacher_hidden,
    head_teacher,
    proto_teacher,
    student_hidden,
    head_student,
    proto_student,
    mask_index,
    mask_count,
):
    toks, protos = lax.axis_size("tok"), lax.axis_size("proto")
    tok, proto = lax.axis_index("tok"), lax.axis_index("proto")
    tok_dev, slots = teacher_hidden.shape[0], student_hidden.shape[0]
    depth = teacher_hidden.shape[1]
    width, local = head_teacher.shape[1], proto_teacher.shape[1]
    lines = local // 128
    share = slots // protos
    core, here = (proto % 2).reshape(1), tok.reshape(1)
    place = jnp.stack([proto, jnp.take(mask_count, tok)])
    dma = pltpu.SemaphoreType.DMA

    up = [(i, (i + 1) % toks) for i in range(toks)]
    down = [(i, (i - 1) % toks) for i in range(toks)]
    rows = proto_teacher.shape[0]

    def hop(pair):
        return lax.ppermute(pair[0], "tok", up), lax.ppermute(pair[1], "tok", down)

    def along(pair, values):
        first, second, values = lax.optimization_barrier((pair[0], pair[1], values))
        return (first, second), values

    chips = protos // 2
    groups = [[2 * k + c for k in range(chips)] for c in range(2)]
    copies, both = call(
        heads_kernel,
        (shaped((chips, depth // protos, 2 * width), bf16), shaped((2 * rows, local), bf16)),
        [HB] * 4,
        (VM, ANY),
        (0, MIB),
        [pltpu.VMEM((depth // protos, width), bf16)] * 2 + [dma((4,))],
    )(head_teacher, head_student, proto_teacher, proto_student)
    mine = exchange(copies, "proto", groups)
    blocks, pair = [both], (both, both)
    pair = hop(pair)
    blocks += list(pair)
    pair, mine = along(pair, mine)
    pair = hop(pair)
    blocks += list(pair)
    other = lax.ppermute(mine, "proto", [(i, i ^ 1) for i in range(protos)])
    pair = hop(pair)
    blocks += list(pair)
    step = 256
    unit_teacher, unit_kept, full_head = call(
        neck_kernel,
        (
            shaped((tok_dev, width), bf16),
            pltpu.HBM((tok_dev, width), bf16),
            pltpu.HBM((chips, depth // chips, width), bf16),
        ),
        [SM, HB, ANY, ANY],
        (VM, HB, HB),
        (2 * tok_dev * depth * width, 10 * MIB),
        [
            pltpu.VMEM((chips, depth // chips, width), bf16),
            pltpu.VMEM((tok_dev // step, step, depth), bf16),
            dma((tok_dev // step + 5,)),
        ],
    )(core, teacher_hidden, mine, other)
    full_head = full_head.reshape(depth, width)
    blocks += list(hop((pair[0][:rows], pair[1][rows:])))

    scores, whole_teacher, whole_student, columns = call(
        scores_kernel,
        (
            pltpu.VMEM((tok_dev, local), bf16),
            pltpu.HBM((toks * rows, local), bf16),
            pltpu.HBM((toks * rows, local), bf16),
            shaped((toks, lines, 128), f32),
        ),
        [SM, VM] + [ANY] * len(blocks),
        (VM, HB, HB, VM),
        (2 * tok_dev * local * width, 12 * MIB),
        [
            pltpu.VMEM((toks * rows, local), bf16),
            pltpu.VMEM((lines, 128), f32),
            dma((2 * len(blocks) + 1,)),
        ],
    )(here, unit_teacher, *blocks)

    row_call = call(
        row_kernel,
        shaped((protos, tok_dev // 128, 128), f32),
        [VM, VM],
        VM,
        (2 * tok_dev * local, 8 * MIB),
        [pltpu.VMEM((tok_dev // 128, 128), f32)],
    )
    column_call = call(
        column_kernel,
        shaped((toks, lines, 128), f32),
        [VM, VM],
        VM,
        (2 * tok_dev * local, 8 * MIB),
        [pltpu.VMEM((tok_dev, 128), f32)],
    )
    for _ in range(2):
        sums = row_call(exchange(columns, "tok"), held(scores))
        columns = column_call(exchange(sums, "proto"), held(scores))
    columns, whole_student = lax.optimization_barrier((columns, whole_student))

    rows = toks * rows
    masked, scale_p, unit_float, norm, grad, soft_total = call(
        student_kernel,
        (
            pltpu.HBM((slots, local), f32),
            pltpu.HBM((8, local), f32),
            pltpu.HBM((slots, width), f32),
            pltpu.HBM((slots, 128), f32),
            pltpu.HBM((slots, width), f32),
            pltpu.HBM((slots, 128), f32),
        ),
        [VM] + [HB] * 5,
        (VM,) * 6,
        (10 * slots * local * width, 8 * MIB),
        [
            pltpu.VMEM((slots, depth), bf16),
            pltpu.VMEM((depth, width), bf16),
            pltpu.VMEM((tok_dev, width), bf16),
            pltpu.VMEM((rows, local), bf16),
            pltpu.VMEM((rows, local), bf16),
            dma((5,)),
        ],
    )(
        mask_index.reshape(1, slots),
        student_hidden,
        full_head,
        unit_kept,
        whole_teacher,
        whole_student,
    )

    parts = call(
        goal_kernel,
        shaped((slots, 2 * width + 128), f32),
        [VM] + [HB] * 5,
        VM,
        (4 * slots * local * width, 4 * MIB),
        [
            pltpu.VMEM((slots, local), f32),
            pltpu.VMEM((8, local), f32),
            pltpu.VMEM((rows, local), bf16),
            pltpu.VMEM((slots, 128), f32),
            dma((3 + 2 * local // 512,)),
        ],
    )(exchange(columns, "tok"), masked, scale_p, whole_student, grad, soft_total)
    parts = exchange(parts.reshape(protos, share, 2 * width + 128), "proto")
    finals = call(
        slots_kernel,
        shaped((protos, 2 * share, width), bf16),
        [SM, VM, HB, HB],
        VM,
        (2 * slots * width, MIB),
        [pltpu.VMEM((share, width), f32), pltpu.VMEM((share, 128), f32), dma((2,))],
    )(place, parts, unit_float, norm)
    hidden_grad, row_loss = call(
        hidden_kernel,
        (shaped(student_hidden.shape, bf16), shaped((1, slots), f32)),
        [VM, VM],
        (VM, VM),
        (2 * slots * width * depth, 3 * MIB),
    )(exchange(finals, "proto"), full_head)
    return (row_loss.reshape(slots), hidden_grad)


def solution(mesh):
    placed = (
        P("tok", None),
        P("proto", None),
        P("tok", "proto"),
        P("tok", None),
        P("proto", None),
        P("tok", "proto"),
        P("tok"),
        P(),
    )
    return jax.shard_map(
        shards, mesh=mesh, in_specs=placed, out_specs=(P("tok"), P("tok", None)), check_vma=False
    )
```

```python
import jax
import jax.numpy as jnp
from jax import lax
from jax.experimental import pallas as pl
from jax.experimental.pallas import tpu as pltpu
from jax.sharding import PartitionSpec as P

teacher_temp = 0.07
student_temp = 0.1
norm_eps = 1e-06
LOG2E = 1.4426950408889634
MIB = 1024 * 1024
f32 = jnp.float32
bf16 = jnp.bfloat16
VM = pl.BlockSpec(memory_space=pltpu.VMEM)
SM = pl.BlockSpec(memory_space=pltpu.SMEM)
HB = pl.BlockSpec(memory_space=pltpu.HBM)
ANY = pl.BlockSpec(memory_space=pl.ANY)
NT = (((1,), (1,)), ((), ()))


def shaped(shape, dtype):
    return jax.ShapeDtypeStruct(shape, dtype)


def call(kernel, out_shape, in_specs, out_specs, cost, scratch=(), mib=40):
    return pl.pallas_call(
        kernel,
        out_shape=out_shape,
        in_specs=in_specs,
        out_specs=out_specs,
        scratch_shapes=list(scratch),
        cost_estimate=pl.CostEstimate(flops=cost[0], bytes_accessed=cost[1], transcendentals=0),
        compiler_params=pltpu.CompilerParams(vmem_limit_bytes=mib * MIB),
    )


def held(values):
    return pltpu.with_memory_space_constraint(values, pltpu.VMEM)


def far(values):
    return pltpu.with_memory_space_constraint(values, pltpu.HBM)


def dot(left, right, dims=(((1,), (0,)), ((), ()))):
    return lax.dot_general(left, right, dims, preferred_element_type=f32)


def split(values):
    high = values.astype(bf16)
    return high, (values - high.astype(f32)).astype(bf16)


def fetch(pairs, sems, first=0):
    copies = [
        pltpu.make_async_copy(source, target, sems.at[first + k])
        for k, (source, target) in enumerate(pairs)
    ]
    for copy in copies:
        copy.start()
    return copies


def settle(copies):
    for copy in copies:
        copy.wait()


def heads_kernel(teacher, student, first, second, copies, both, v_teacher, v_student, sems):
    rows, width = first.shape[0], teacher.shape[1]
    heads = fetch([(teacher, v_teacher), (student, v_student)], sems)
    rest = fetch(
        [(first, both.at[pl.ds(0, rows), :]), (second, both.at[pl.ds(rows, rows), :])], sems, 2
    )
    settle(heads)
    copies[:, :, :width] = jnp.broadcast_to(v_teacher[...][None], copies.shape[:2] + (width,))
    copies[:, :, width:] = jnp.broadcast_to(v_student[...][None], copies.shape[:2] + (width,))
    settle(rest)


def stage_kernel(hidden, staged, sems):
    step = hidden.shape[0] // 4
    rows = [pl.ds(k * step, step) for k in range(4)]
    settle(fetch([(hidden.at[at, :], staged.at[at, :]) for at in rows], sems))


def neck_kernel(core, hidden, mine, other, unit, student, head, full, sems):
    chips, rows, double = mine.shape
    width = double // 2
    for chip in range(chips):
        at = 2 * rows * chip
        near = pl.ds(pl.multiple_of(at + core[0] * rows, rows), rows)
        away = pl.ds(pl.multiple_of(at + (1 - core[0]) * rows, rows), rows)
        head[near, :] = mine[chip, :, :width]
        head[away, :] = other[chip, :, :width]
        full[near, :] = mine[chip, :, width:]
        full[away, :] = other[chip, :, width:]
    copies = fetch([(full, student)], sems)
    step = 256
    for k in range(hidden.shape[0] // step):
        at = slice(k * step, (k + 1) * step)
        neck = dot(hidden[at, :], head[...])
        scale = lax.rsqrt(jnp.sum(neck * neck, axis=1, keepdims=True) + norm_eps)
        unit[at, :] = (neck * scale).astype(bf16)
    settle(copies)


def join_kernel(mine, other, teacher, student):
    rows = mine.shape[0] // 2
    teacher[:rows, :] = mine[:rows, :]
    teacher[rows:, :] = other[:rows, :]
    student[:rows, :] = mine[rows:, :]
    student[rows:, :] = other[rows:, :]


def place_blocks(here, own, came, crossed, whole):
    rows = own.shape[0]
    count = whole.shape[0] // rows
    way = 1 - 2 * here[1]

    def put(steps, block):
        origin = lax.rem(here[0] + way * steps + count, count) * rows
        whole[pl.ds(pl.multiple_of(origin, rows), rows), :] = block[:rows, :]

    put(0, own)
    for k, block in enumerate(came):
        put(-(k + 1), block)
    for k, block in enumerate(crossed):
        put(k + 1, block)


def scores_kernel(here, unit, own, *refs):
    blocks, refs = refs[:-7], refs[-7:]
    scores, teacher, kept, columns, whole, sums, sems = refs
    hops = (len(blocks) + 1) // 2
    place_blocks(here, own[: own.shape[0] // 2, :], blocks[:hops], blocks[hops:], whole)
    rest = fetch([(whole, teacher), (unit, kept)], sems)
    fold = LOG2E / teacher_temp
    step = 256
    count = step // 128

    def over_columns(c, _):
        at = pl.ds(pl.multiple_of(c * step, step), step)
        weights = whole[:, at]
        acc = jnp.zeros((8, step), f32)
        for r in range(unit.shape[0] // step):
            rows = slice(r * step, (r + 1) * step)
            value = jnp.exp2(dot(unit[rows, :], weights) * fold)
            scores[rows, at] = value.astype(bf16)
            acc = acc + jnp.sum(value.reshape(step // 8, 8, step), axis=0)
        acc = jnp.sum(acc, axis=0, keepdims=True)
        for k in range(count):
            sums[pl.ds(c * count + k, 1), :] = acc[:, k * 128 : (k + 1) * 128]
        return 0

    lax.fori_loop(0, whole.shape[1] // step, over_columns, 0)
    settle(rest)
    columns[...] = jnp.broadcast_to(sums[...][None], columns.shape)


def row_kernel(parts, scores, rows, sums):
    inverse = 1.0 / jnp.sum(parts[...], axis=0)
    group = 4

    def over_rows(i, _):
        for r in range(group):
            at = pl.ds(pl.multiple_of(i * (group * 128) + r * 128, 128), 128)
            acc = jnp.zeros((128, 128), f32)
            for c in range(scores.shape[1] // 128):
                block = scores[at, c * 128 : (c + 1) * 128].astype(f32)
                acc = acc + block * inverse[c : c + 1, :]
            sums[pl.ds(i * group + r, 1), :] = jnp.sum(acc.T, axis=0, keepdims=True)
        return 0

    lax.fori_loop(0, scores.shape[0] // (group * 128), over_rows, 0)
    rows[...] = jnp.broadcast_to(sums[...].astype(rows.dtype)[None], rows.shape)


def column_kernel(parts, scores, columns, weight):
    turned = (1.0 / jnp.sum(parts[...].astype(f32), axis=0)).T
    for r in range(weight.shape[0] // 128):
        weight[r * 128 : (r + 1) * 128, :] = jnp.broadcast_to(turned[:, r : r + 1], (128, 128))
    step = 64
    tiles = scores.shape[1] // 128

    def over_rows(r, acc):
        at = pl.ds(pl.multiple_of(r * step, step), step)
        w = weight[at, :]
        out = []
        for c in range(tiles):
            block = scores[at, c * 128 : (c + 1) * 128].astype(f32) * w
            out.append(acc[c] + jnp.sum(block.reshape(step // 8, 8, 128), axis=0))
        return tuple(out)

    zeros = tuple(jnp.zeros((8, 128), f32) for _ in range(tiles))
    acc = lax.fori_loop(0, scores.shape[0] // step, over_rows, zeros, unroll=4)
    total = jnp.concatenate([jnp.sum(a, axis=0, keepdims=True) for a in acc], axis=0)
    columns[...] = jnp.broadcast_to(total[None], columns.shape)


def last_column_kernel(here, parts, scores, own, *refs):
    blocks, (columns, student, whole, weight, sems) = refs[:-5], refs[-5:]
    hops = (len(blocks) + 1) // 2
    place_blocks(here, own[own.shape[0] // 2 :, :], blocks[:hops], blocks[hops:], whole)
    copies = fetch([(whole, student)], sems)
    column_kernel(parts, scores, columns, weight)
    settle(copies)


def student_kernel(index, hidden, head, unit, teacher, student, *refs):
    masked, scale_out, unit_out, norm, grad, total = refs[:6]
    v_hidden, v_head, v_unit, v_teacher, whole, sems = refs[6:]
    copies = fetch(
        [
            (hidden, v_hidden),
            (head, v_head),
            (unit, v_unit),
            (teacher, v_teacher),
            (student, whole),
        ],
        sems,
    )
    slots, tokens = v_hidden.shape[0], v_unit.shape[0]
    settle(copies[:2])
    neck = dot(v_hidden[...], v_head[...])
    scale = lax.rsqrt(jnp.sum(neck * neck, axis=1, keepdims=True) + norm_eps)
    unit_float = neck * scale
    unit_out[...] = unit_float
    norm[...] = jnp.broadcast_to(scale, norm.shape)
    student = unit_float.astype(bf16)
    settle(copies[2:])
    wanted = jnp.broadcast_to(index[...].astype(f32), (128, slots)).T[:, 0:1]
    chosen = wanted == lax.broadcasted_iota(jnp.int32, (slots, tokens), 1).astype(f32)
    picked = dot(chosen.astype(f32).astype(bf16), v_unit[...]).astype(bf16)
    fold = LOG2E / teacher_temp
    step = 256
    grad_acc = jnp.zeros(grad.shape, f32)
    total_acc = jnp.zeros((slots, 1), f32)
    for c in range(whole.shape[1] // step):
        at = slice(c * step, (c + 1) * step)
        masked[:, at] = jnp.exp2(dot(picked, v_teacher[:, at]) * fold)
        weights = whole[:, at]
        wide = weights.astype(f32)
        scale_p = lax.rsqrt(jnp.sum(wide * wide, axis=0, keepdims=True) + norm_eps) / student_temp
        scale_out[:, at] = jnp.broadcast_to(scale_p, (8, step))
        soft = jnp.exp2(dot(student, weights) * (scale_p * LOG2E))
        total_acc = total_acc + jnp.sum(soft, axis=1, keepdims=True)
        high, low = split(soft * scale_p)
        grad_acc = grad_acc + dot(high, weights, NT) + dot(low, weights, NT)
    grad[...] = grad_acc
    total[...] = jnp.broadcast_to(total_acc, total.shape)


def goal_kernel(
    parts, masked, scale_p, whole, grad, total, out, v_masked, v_scale, v_whole, v_total, sems
):
    slots, width = grad.shape
    step = 512
    count = whole.shape[1] // step
    copies = fetch([(scale_p, v_scale), (total, v_total), (grad, out.at[:, :width])], sems)
    blocks = []
    for c in range(count):
        at = pl.ds(c * step, step)
        blocks.append(
            fetch(
                [(masked.at[:, at], v_masked.at[:, at]), (whole.at[:, at], v_whole.at[:, at])],
                sems,
                3 + 2 * c,
            )
        )
    inverse = 1.0 / jnp.sum(parts[...], axis=0)
    grad_acc = jnp.zeros((slots, width), f32)
    goal_acc = jnp.zeros((slots, 128), f32)
    settle(copies[:1])
    for c in range(count):
        settle(blocks[c])
        pieces = []
        for k in range(c * (step // 128), (c + 1) * (step // 128)):
            at = slice(k * 128, (k + 1) * 128)
            goal = v_masked[:, at] * inverse[k : k + 1, :]
            goal_acc = goal_acc + goal
            pieces.append(goal * v_scale[0:1, at])
        high, low = split(jnp.concatenate(pieces, axis=1))
        weights = v_whole[:, c * step : (c + 1) * step]
        grad_acc = grad_acc + dot(high, weights, NT) + dot(low, weights, NT)
    out[:, width : 2 * width] = grad_acc
    goal_total = jnp.sum(goal_acc, axis=1, keepdims=True)
    lane = lax.broadcasted_iota(jnp.int32, (slots, 128), 1)
    settle(copies[1:])
    out[:, 2 * width :] = jnp.where(lane == 0, v_total[...], goal_total)


def slots_kernel(place, parts, unit_float, norm, out, v_unit, v_norm, sems):
    share, width = parts.shape[1], unit_float.shape[1]
    at = pl.multiple_of(place[0] * share, share)
    copies = fetch(
        [(unit_float.at[pl.ds(at, share), :], v_unit), (norm.at[pl.ds(at, share), :], v_norm)], sems
    )
    mine = jnp.sum(parts[...], axis=0)
    settle(copies)
    unit = v_unit[...]
    scale = v_norm[:, 0:1]
    soft_total = mine[:, 2 * width : 2 * width + 1]
    goal_total = mine[:, 2 * width + 1 : 2 * width + 2]
    soft, goal = mine[:, :width] / soft_total, mine[:, width : 2 * width] / goal_total
    slot = at + lax.broadcasted_iota(jnp.int32, (share, 1), 0)
    live = jnp.where(slot < place[1], 1.0, 0.0)
    target_dot = jnp.sum(unit.astype(bf16).astype(f32) * goal, axis=1, keepdims=True)
    loss = live * (jnp.log(soft_total) - target_dot)
    unit_grad = live * (soft - goal)
    inner = jnp.sum(unit * unit_grad, axis=1, keepdims=True)
    neck_grad = scale * (unit_grad - unit * inner)
    top = loss.astype(bf16).astype(f32)
    mid = (loss - top).astype(bf16).astype(f32)
    low = loss - top - mid
    lane = lax.broadcasted_iota(jnp.int32, (share, width), 1)
    tail = jnp.where(lane == 0, top, jnp.where(lane == 1, mid, jnp.where(lane == 2, low, 0.0)))
    both = jnp.concatenate([neck_grad, tail], axis=0).astype(bf16)
    out[...] = jnp.broadcast_to(both[None], out.shape)


def hidden_kernel(parts, head, hidden, loss):
    count, double, width = parts.shape
    share = double // 2
    wide = parts[...].astype(f32)
    neck_grad = wide[:, :share, :].reshape(count * share, width).astype(bf16)
    tail = wide[:, share:, :128].reshape(count * share, 128).T
    loss[...] = tail[0:1, :] + tail[1:2, :] + tail[2:3, :]
    step = 512
    for c in range(head.shape[0] // step):
        at = slice(c * step, (c + 1) * step)
        hidden[:, at] = dot(neck_grad, head[at, :], NT).astype(bf16)


def exchange(blocks, axis, groups=None):
    return lax.all_to_all(blocks, axis, 0, 0, tiled=True, axis_index_groups=groups)


def shards(
    teacher_hidden,
    head_teacher,
    proto_teacher,
    student_hidden,
    head_student,
    proto_student,
    mask_index,
    mask_count,
):
    toks, protos = lax.axis_size("tok"), lax.axis_size("proto")
    tok, proto = lax.axis_index("tok"), lax.axis_index("proto")
    tok_dev, slots = teacher_hidden.shape[0], student_hidden.shape[0]
    depth = teacher_hidden.shape[1]
    width, local = head_teacher.shape[1], proto_teacher.shape[1]
    lines = local // 128
    share = slots // protos
    core, here = (proto % 2).reshape(1), jnp.stack([tok, proto % 2])
    place = jnp.stack([proto, jnp.take(mask_count, tok)])
    dma = pltpu.SemaphoreType.DMA

    swap = [(i, i ^ 1) for i in range(protos)]
    along = []
    for t in range(toks):
        for p in range(protos):
            to = (t + (1 if p % 2 == 0 else -1)) % toks
            along.append((t * protos + p, to * protos + p))
    rows = proto_teacher.shape[0]

    chips = protos // 2
    groups = [[2 * k + c for k in range(chips)] for c in range(2)]
    copies, both = call(
        heads_kernel,
        (shaped((chips, depth // protos, 2 * width), bf16), shaped((2 * rows, local), bf16)),
        [HB] * 4,
        (VM, VM),
        (0, MIB),
        [pltpu.VMEM((depth // protos, width), bf16)] * 2 + [dma((4,))],
    )(far(head_teacher), far(head_student), far(proto_teacher), far(proto_student))
    mine = exchange(copies, "proto", groups)
    sibling = lax.ppermute(both, "proto", swap)
    chains = call(
        join_kernel,
        (shaped((2 * rows, local), bf16),) * 2,
        [VM, VM],
        (VM, VM),
        (0, MIB),
    )(both, sibling)
    teacher_own, student_own = chains
    hops = toks // 2
    hidden = teacher_hidden
    came, crossed = [], []
    for hop in range(hops):
        sent = came[-1] if hop else teacher_own
        came.append(lax.ppermute(sent if hop < hops - 1 else sent[:rows], ("tok", "proto"), along))
        if hop < hops - 1:
            crossed.append(lax.ppermute(came[-1][rows:], "proto", swap))
        if hop == 1:
            hidden, mine, _ = lax.optimization_barrier((hidden, mine, came[-1]))
            other = lax.ppermute(mine, "proto", swap)
        if hop == hops - 2:
            student_own, _ = lax.optimization_barrier((student_own, came[-1]))
    late, late_crossed = [lax.ppermute(student_own, ("tok", "proto"), along)], []
    staged = call(
        stage_kernel,
        pltpu.VMEM(hidden.shape, bf16),
        [HB],
        VM,
        (0, 16 * MIB),
        [dma((4,))],
    )(far(hidden))
    unit_teacher, full_head = call(
        neck_kernel,
        (shaped((tok_dev, width), bf16), pltpu.HBM((depth, width), bf16)),
        [SM, VM, VM, VM],
        (VM, HB),
        (2 * tok_dev * depth * width, 10 * MIB),
        [pltpu.VMEM((depth, width), bf16), pltpu.VMEM((depth, width), bf16), dma((1,))],
    )(core, held(staged), mine, other)

    blocks = came + crossed
    scores, whole_teacher, unit_kept, columns = call(
        scores_kernel,
        (
            pltpu.VMEM((tok_dev, local), bf16),
            pltpu.HBM((toks * rows, local), bf16),
            pltpu.HBM((tok_dev, width), bf16),
            shaped((toks, lines, 128), f32),
        ),
        [SM] + [VM] * (2 + len(blocks)),
        (VM, HB, HB, VM),
        (2 * tok_dev * local * width, 12 * MIB),
        [
            pltpu.VMEM((toks * rows, local), bf16),
            pltpu.VMEM((lines, 128), f32),
            dma((2,)),
        ],
    )(here, unit_teacher, both, *blocks)

    row_call = call(
        row_kernel,
        shaped((protos, tok_dev // 128, 128), bf16),
        [VM, VM],
        VM,
        (2 * tok_dev * local, 8 * MIB),
        [pltpu.VMEM((tok_dev // 128, 128), f32)],
    )
    column_call = call(
        column_kernel,
        shaped((toks, lines, 128), f32),
        [VM, VM],
        VM,
        (2 * tok_dev * local, 8 * MIB),
        [pltpu.VMEM((tok_dev, 128), f32)],
    )
    last_column_call = call(
        last_column_kernel,
        (shaped((toks, lines, 128), f32), pltpu.HBM((toks * rows, local), bf16)),
        [SM] + [VM] * (2 + 2 * hops),
        (VM, HB),
        (2 * tok_dev * local, 8 * MIB),
        [
            pltpu.VMEM((toks * rows, local), bf16),
            pltpu.VMEM((tok_dev, 128), f32),
            dma((1,)),
        ],
    )

    def onward(values):
        values, late[-1], *late_crossed[:] = lax.optimization_barrier(
            (values, late[-1], *late_crossed)
        )
        if len(late) < hops:
            late_crossed.append(lax.ppermute(late[-1][rows:], "proto", swap))
            sent = late[-1] if len(late) < hops - 1 else late[-1][:rows]
            late.append(lax.ppermute(sent, ("tok", "proto"), along))
        return values

    columns = onward(columns)
    sums = row_call(exchange(columns, "tok"), held(scores))
    sums = onward(sums)
    columns = column_call(exchange(sums, "proto"), held(scores))
    columns = onward(columns)
    sums = row_call(exchange(columns, "tok"), held(scores))
    sums = onward(sums)
    columns, whole_student = last_column_call(
        here, exchange(sums, "proto"), held(scores), both, *late, *late_crossed
    )
    columns, whole_student = lax.optimization_barrier((columns, whole_student))

    rows = toks * rows
    masked, scale_p, unit_float, norm, grad, soft_total = call(
        student_kernel,
        (
            pltpu.HBM((slots, local), f32),
            pltpu.HBM((8, local), f32),
            pltpu.HBM((slots, width), f32),
            pltpu.HBM((slots, 128), f32),
            pltpu.HBM((slots, width), f32),
            pltpu.HBM((slots, 128), f32),
        ),
        [VM] + [HB] * 5,
        (VM,) * 6,
        (10 * slots * local * width, 8 * MIB),
        [
            pltpu.VMEM((slots, depth), bf16),
            pltpu.VMEM((depth, width), bf16),
            pltpu.VMEM((tok_dev, width), bf16),
            pltpu.VMEM((rows, local), bf16),
            pltpu.VMEM((rows, local), bf16),
            dma((5,)),
        ],
    )(
        mask_index.reshape(1, slots),
        far(student_hidden),
        far(full_head),
        far(unit_kept),
        far(whole_teacher),
        far(whole_student),
    )

    parts = call(
        goal_kernel,
        shaped((slots, 2 * width + 128), f32),
        [VM] + [HB] * 5,
        VM,
        (4 * slots * local * width, 4 * MIB),
        [
            pltpu.VMEM((slots, local), f32),
            pltpu.VMEM((8, local), f32),
            pltpu.VMEM((rows, local), bf16),
            pltpu.VMEM((slots, 128), f32),
            dma((3 + 2 * local // 512,)),
        ],
    )(
        exchange(columns, "tok"),
        far(masked),
        far(scale_p),
        far(whole_student),
        far(grad),
        far(soft_total),
    )
    parts = exchange(parts.reshape(protos, share, 2 * width + 128), "proto")
    finals = call(
        slots_kernel,
        shaped((protos, 2 * share, width), bf16),
        [SM, VM, HB, HB],
        VM,
        (2 * slots * width, MIB),
        [pltpu.VMEM((share, width), f32), pltpu.VMEM((share, 128), f32), dma((2,))],
    )(place, parts, far(unit_float), far(norm))
    hidden_grad, row_loss = call(
        hidden_kernel,
        (shaped(student_hidden.shape, bf16), shaped((1, slots), f32)),
        [VM, VM],
        (VM, VM),
        (2 * slots * width * depth, 3 * MIB),
    )(exchange(finals, "proto"), full_head)
    return (row_loss.reshape(slots), hidden_grad)


def solution(mesh):
    placed = (
        P("tok", None),
        P("proto", None),
        P("tok", "proto"),
        P("tok", None),
        P("proto", None),
        P("tok", "proto"),
        P("tok"),
        P(),
    )
    return jax.shard_map(
        shards, mesh=mesh, in_specs=placed, out_specs=(P("tok"), P("tok", None)), check_vma=False
    )
```

```python
import jax
import jax.numpy as jnp
from jax import lax
from jax.experimental import pallas as pl
from jax.experimental.pallas import tpu as pltpu
from jax.sharding import PartitionSpec as P

teacher_temp = 0.07
student_temp = 0.1
norm_eps = 1e-06
LOG2E = 1.4426950408889634
MIB = 1024 * 1024
f32 = jnp.float32
bf16 = jnp.bfloat16
VM = pl.BlockSpec(memory_space=pltpu.VMEM)
SM = pl.BlockSpec(memory_space=pltpu.SMEM)
HB = pl.BlockSpec(memory_space=pltpu.HBM)
ANY = pl.BlockSpec(memory_space=pl.ANY)
NT = (((1,), (1,)), ((), ()))


def shaped(shape, dtype):
    return jax.ShapeDtypeStruct(shape, dtype)


def call(kernel, out_shape, in_specs, out_specs, cost, scratch=(), mib=40):
    return pl.pallas_call(
        kernel,
        out_shape=out_shape,
        in_specs=in_specs,
        out_specs=out_specs,
        scratch_shapes=list(scratch),
        cost_estimate=pl.CostEstimate(flops=cost[0], bytes_accessed=cost[1], transcendentals=0),
        compiler_params=pltpu.CompilerParams(vmem_limit_bytes=mib * MIB),
    )


def held(values):
    return pltpu.with_memory_space_constraint(values, pltpu.VMEM)


def far(values):
    return pltpu.with_memory_space_constraint(values, pltpu.HBM)


def dot(left, right, dims=(((1,), (0,)), ((), ()))):
    return lax.dot_general(left, right, dims, preferred_element_type=f32)


def split(values):
    high = values.astype(bf16)
    return high, (values - high.astype(f32)).astype(bf16)


def fetch(pairs, sems, first=0):
    copies = [
        pltpu.make_async_copy(source, target, sems.at[first + k])
        for k, (source, target) in enumerate(pairs)
    ]
    for copy in copies:
        copy.start()
    return copies


def settle(copies):
    for copy in copies:
        copy.wait()


def heads_kernel(teacher, student, first, second, copies, both, v_teacher, v_student, sems):
    rows, width = first.shape[0], teacher.shape[1]
    heads = fetch([(teacher, v_teacher), (student, v_student)], sems)
    rest = fetch(
        [(first, both.at[pl.ds(0, rows), :]), (second, both.at[pl.ds(rows, rows), :])], sems, 2
    )
    settle(heads)
    copies[:, :, :width] = jnp.broadcast_to(v_teacher[...][None], copies.shape[:2] + (width,))
    copies[:, :, width:] = jnp.broadcast_to(v_student[...][None], copies.shape[:2] + (width,))
    settle(rest)


def stage_kernel(hidden, staged, sems):
    step = hidden.shape[0] // 4
    rows = [pl.ds(k * step, step) for k in range(4)]
    settle(fetch([(hidden.at[at, :], staged.at[at, :]) for at in rows], sems))


def neck_kernel(here, hidden, mine, other, unit, student, head, full, sems):
    chips, rows, double = mine.shape
    width = double // 2
    for chip in range(chips):
        at = 2 * rows * chip
        near = pl.ds(pl.multiple_of(at + here[1] * rows, rows), rows)
        away = pl.ds(pl.multiple_of(at + (1 - here[1]) * rows, rows), rows)
        head[near, :] = mine[chip, :, :width]
        head[away, :] = other[chip, :, :width]
        full[near, :] = mine[chip, :, width:]
        full[away, :] = other[chip, :, width:]
    copies = fetch([(full, student)], sems)
    step = 256
    for k in range(hidden.shape[0] // step):
        at = slice(k * step, (k + 1) * step)
        neck = dot(hidden[at, :], head[...])
        scale = lax.rsqrt(jnp.sum(neck * neck, axis=1, keepdims=True) + norm_eps)
        unit[at, :] = (neck * scale).astype(bf16)
    settle(copies)


def join_kernel(mine, other, teacher, student):
    rows = mine.shape[0] // 2
    teacher[:rows, :] = mine[:rows, :]
    teacher[rows:, :] = other[:rows, :]
    student[:rows, :] = mine[rows:, :]
    student[rows:, :] = other[rows:, :]


def place_blocks(here, own, came, crossed, whole):
    rows = own.shape[0]
    count = whole.shape[0] // rows
    way = 1 - 2 * here[1]

    def put(steps, block):
        origin = lax.rem(here[0] + way * steps + count, count) * rows
        whole[pl.ds(pl.multiple_of(origin, rows), rows), :] = block[:rows, :]

    put(0, own)
    for k, block in enumerate(came):
        put(-(k + 1), block)
    for k, block in enumerate(crossed):
        put(k + 1, block)


def scores_kernel(here, unit, own, *refs):
    blocks, refs = refs[:-7], refs[-7:]
    scores, teacher, kept, columns, whole, sums, sems = refs
    hops = (len(blocks) + 1) // 2
    place_blocks(here, own[: own.shape[0] // 2, :], blocks[:hops], blocks[hops:], whole)
    rest = fetch([(whole, teacher), (unit, kept)], sems)
    fold = LOG2E / teacher_temp
    step = 256
    count = step // 128

    def over_columns(c, _):
        at = pl.ds(pl.multiple_of(c * step, step), step)
        weights = whole[:, at]
        acc = jnp.zeros((8, step), f32)
        for r in range(unit.shape[0] // step):
            rows = slice(r * step, (r + 1) * step)
            value = jnp.exp2(dot(unit[rows, :], weights) * fold)
            scores[rows, at] = value.astype(bf16)
            acc = acc + jnp.sum(value.reshape(step // 8, 8, step), axis=0)
        acc = jnp.sum(acc, axis=0, keepdims=True)
        for k in range(count):
            sums[pl.ds(c * count + k, 1), :] = acc[:, k * 128 : (k + 1) * 128]
        return 0

    lax.fori_loop(0, whole.shape[1] // step, over_columns, 0)
    settle(rest)
    columns[...] = jnp.broadcast_to(sums[...][None], columns.shape)


def row_kernel(parts, scores, rows, sums):
    inverse = 1.0 / jnp.sum(parts[...], axis=0)
    group = 4

    def over_rows(i, _):
        for r in range(group):
            at = pl.ds(pl.multiple_of(i * (group * 128) + r * 128, 128), 128)
            acc = jnp.zeros((128, 128), f32)
            for c in range(scores.shape[1] // 128):
                block = scores[at, c * 128 : (c + 1) * 128].astype(f32)
                acc = acc + block * inverse[c : c + 1, :]
            sums[pl.ds(i * group + r, 1), :] = jnp.sum(acc.T, axis=0, keepdims=True)
        return 0

    lax.fori_loop(0, scores.shape[0] // (group * 128), over_rows, 0)
    rows[...] = jnp.broadcast_to(sums[...].astype(rows.dtype)[None], rows.shape)


def column_kernel(parts, scores, columns, weight):
    turned = (1.0 / jnp.sum(parts[...].astype(f32), axis=0)).T
    for r in range(weight.shape[0] // 128):
        weight[r * 128 : (r + 1) * 128, :] = jnp.broadcast_to(turned[:, r : r + 1], (128, 128))
    step = 64
    tiles = scores.shape[1] // 128

    def over_rows(r, acc):
        at = pl.ds(pl.multiple_of(r * step, step), step)
        w = weight[at, :]
        out = []
        for c in range(tiles):
            block = scores[at, c * 128 : (c + 1) * 128].astype(f32) * w
            out.append(acc[c] + jnp.sum(block.reshape(step // 8, 8, 128), axis=0))
        return tuple(out)

    zeros = tuple(jnp.zeros((8, 128), f32) for _ in range(tiles))
    acc = lax.fori_loop(0, scores.shape[0] // step, over_rows, zeros, unroll=4)
    total = jnp.concatenate([jnp.sum(a, axis=0, keepdims=True) for a in acc], axis=0)
    columns[...] = jnp.broadcast_to(total[None], columns.shape)


def last_column_kernel(here, parts, scores, own, *refs):
    blocks, (columns, student, whole, weight, sems) = refs[:-5], refs[-5:]
    hops = (len(blocks) + 1) // 2
    place_blocks(here, own[own.shape[0] // 2 :, :], blocks[:hops], blocks[hops:], whole)
    copies = fetch([(whole, student)], sems)
    column_kernel(parts, scores, columns, weight)
    settle(copies)


def student_kernel(index, hidden, head, unit, teacher, student, *refs):
    masked, scale_out, unit_out, grad, total = refs[:5]
    v_hidden, v_head, v_unit, v_teacher, whole, sems = refs[5:]
    copies = fetch(
        [
            (hidden, v_hidden),
            (head, v_head),
            (unit, v_unit),
            (teacher, v_teacher),
            (student, whole),
        ],
        sems,
    )
    slots, tokens = v_hidden.shape[0], v_unit.shape[0]
    settle(copies[:2])
    neck = dot(v_hidden[...], v_head[...])
    scale = lax.rsqrt(jnp.sum(neck * neck, axis=1, keepdims=True) + norm_eps)
    unit_float = neck * scale
    width = v_head.shape[1]
    unit_out[:, :width] = unit_float
    unit_out[:, width:] = jnp.broadcast_to(scale, (unit_float.shape[0], 128))
    student = unit_float.astype(bf16)
    settle(copies[2:])
    wanted = jnp.broadcast_to(index[...].astype(f32), (128, slots)).T[:, 0:1]
    chosen = wanted == lax.broadcasted_iota(jnp.int32, (slots, tokens), 1).astype(f32)
    picked = dot(chosen.astype(f32).astype(bf16), v_unit[...]).astype(bf16)
    fold = LOG2E / teacher_temp
    step = 256
    grad_acc = jnp.zeros(grad.shape, f32)
    total_acc = jnp.zeros((slots, 1), f32)
    for c in range(whole.shape[1] // step):
        at = slice(c * step, (c + 1) * step)
        masked[:, at] = jnp.exp2(dot(picked, v_teacher[:, at]) * fold)
        weights = whole[:, at]
        wide = weights.astype(f32)
        scale_p = lax.rsqrt(jnp.sum(wide * wide, axis=0, keepdims=True) + norm_eps) / student_temp
        scale_out[:, at] = jnp.broadcast_to(scale_p, (8, step))
        soft = jnp.exp2(dot(student, weights) * (scale_p * LOG2E))
        total_acc = total_acc + jnp.sum(soft, axis=1, keepdims=True)
        high, low = split(soft * scale_p)
        grad_acc = grad_acc + dot(high, weights, NT) + dot(low, weights, NT)
    grad[...] = grad_acc
    total[...] = jnp.broadcast_to(total_acc, total.shape)


def goal_kernel(parts, masked, unit, scale_p, whole, grad, total, out, v_scale, v_whole, v_total, sems):
    slots, width = grad.shape
    step = 512
    count = whole.shape[1] // step
    copies = fetch([(scale_p, v_scale), (total, v_total), (grad, out.at[:, :width])], sems)
    blocks = [pl.ds(c * step, step) for c in range(count)]
    blocks = fetch([(whole.at[:, at], v_whole.at[:, at]) for at in blocks], sems, 3)
    inverse = 1.0 / jnp.sum(parts[...], axis=0)
    grad_acc = jnp.zeros((slots, width), f32)
    goal_acc = jnp.zeros((slots, 128), f32)
    settle(copies[:1])
    for c in range(count):
        pieces = []
        for k in range(c * (step // 128), (c + 1) * (step // 128)):
            at = slice(k * 128, (k + 1) * 128)
            goal = masked[:, at] * inverse[k : k + 1, :]
            goal_acc = goal_acc + goal
            pieces.append(goal * v_scale[0:1, at])
        high, low = split(jnp.concatenate(pieces, axis=1))
        blocks[c].wait()
        weights = v_whole[:, c * step : (c + 1) * step]
        grad_acc = grad_acc + dot(high, weights, NT) + dot(low, weights, NT)
    out[:, width : 2 * width] = grad_acc
    goal_total = jnp.sum(goal_acc, axis=1, keepdims=True)
    rounded = unit[:, :width].astype(bf16).astype(f32)
    goal_dot = jnp.sum(rounded * grad_acc, axis=1, keepdims=True)
    lane = lax.broadcasted_iota(jnp.int32, (slots, 128), 1)
    settle(copies[1:])
    sums = jnp.where(lane == 0, v_total[...], jnp.where(lane == 1, goal_total, goal_dot)).T
    rows = [sums[k : k + 1, c : c + 128] for k in range(3) for c in range(0, slots, 128)]
    tile = jnp.concatenate(rows + [jnp.zeros((8 - len(rows), 128), f32)], axis=0)
    out[:, 2 * width :] = jnp.broadcast_to(tile[None], (slots // 8, 8, 128)).reshape(slots, 128)


def slots_kernel(here, counts, parts, unit_float, out, loss):
    count = counts[here[0]]
    share, width = parts.shape[1], unit_float.shape[1] - 128
    mine = jnp.sum(parts[...], axis=0)
    sums = mine[:, 2 * width :]
    slot = 128 * lax.broadcasted_iota(jnp.int32, (2, 128), 0)
    slot = slot + lax.broadcasted_iota(jnp.int32, (2, 128), 1)
    live = jnp.where(slot < count, 1.0, 0.0)
    loss[...] = live * (jnp.log(sums[0:2, :]) - sums[4:6, :] / sums[2:4, :])
    at = pl.multiple_of(here[2] * share, share)
    row = lax.div(at, 128)
    pick = lax.broadcasted_iota(jnp.int32, (share, 128), 1) == (
        lax.rem(at, 128) + lax.broadcasted_iota(jnp.int32, (share, 128), 0)
    )

    def column(first, second):
        line = jnp.where(row == 0, first, second)
        return jnp.sum(jnp.where(pick, line, 0.0), axis=1, keepdims=True)

    soft_total = column(sums[0:1, :], sums[1:2, :])
    goal_total = column(sums[2:3, :], sums[3:4, :])
    unit = unit_float[pl.ds(at, share), :width]
    scale = unit_float[pl.ds(at, share), width : width + 1]
    soft, goal = mine[:, :width] / soft_total, mine[:, width : 2 * width] / goal_total
    slot = at + lax.broadcasted_iota(jnp.int32, (share, 1), 0)
    unit_grad = jnp.where(slot < count, soft - goal, 0.0)
    inner = jnp.sum(unit * unit_grad, axis=1, keepdims=True)
    neck_grad = scale * (unit_grad - unit * inner)
    halves = jnp.concatenate([neck_grad[:, : width // 2], neck_grad[:, width // 2 :]], axis=0)
    out[...] = jnp.broadcast_to(halves.astype(bf16)[None], out.shape)


def hidden_kernel(parts, head, hidden):
    count, double, half = parts.shape
    share = double // 2
    wide = parts[...].astype(f32)
    halves = [
        wide[:, k * share : (k + 1) * share, :].reshape(count * share, half) for k in range(2)
    ]
    neck_grad = jnp.concatenate(halves, axis=1).astype(bf16)
    step = 512
    for c in range(head.shape[0] // step):
        at = slice(c * step, (c + 1) * step)
        hidden[:, at] = dot(neck_grad, head[at, :], NT).astype(bf16)


def exchange(blocks, axis, groups=None):
    return lax.all_to_all(blocks, axis, 0, 0, tiled=True, axis_index_groups=groups)


def shards(
    teacher_hidden,
    head_teacher,
    proto_teacher,
    student_hidden,
    head_student,
    proto_student,
    mask_index,
    mask_count,
):
    toks, protos = lax.axis_size("tok"), lax.axis_size("proto")
    tok, proto = lax.axis_index("tok"), lax.axis_index("proto")
    tok_dev, slots = teacher_hidden.shape[0], student_hidden.shape[0]
    depth = teacher_hidden.shape[1]
    width, local = head_teacher.shape[1], proto_teacher.shape[1]
    lines = local // 128
    share = slots // protos
    here = jnp.stack([tok, proto % 2, proto])
    dma = pltpu.SemaphoreType.DMA

    swap = [(i, i ^ 1) for i in range(protos)]
    along = []
    for t in range(toks):
        for p in range(protos):
            to = (t + (1 if p % 2 == 0 else -1)) % toks
            along.append((t * protos + p, to * protos + p))
    rows = proto_teacher.shape[0]

    chips = protos // 2
    groups = [[2 * k + c for k in range(chips)] for c in range(2)]
    copies, both = call(
        heads_kernel,
        (shaped((chips, depth // protos, 2 * width), bf16), shaped((2 * rows, local), bf16)),
        [HB] * 4,
        (VM, VM),
        (0, MIB),
        [pltpu.VMEM((depth // protos, width), bf16)] * 2 + [dma((4,))],
    )(far(head_teacher), far(head_student), far(proto_teacher), far(proto_student))
    mine = exchange(copies, "proto", groups)
    sibling = lax.ppermute(both, "proto", swap)
    chains = call(
        join_kernel,
        (shaped((2 * rows, local), bf16),) * 2,
        [VM, VM],
        (VM, VM),
        (0, MIB),
    )(both, sibling)
    teacher_own, student_own = chains
    hops = toks // 2
    hidden = teacher_hidden
    came, crossed = [], []
    for hop in range(hops):
        sent = came[-1] if hop else teacher_own
        came.append(lax.ppermute(sent if hop < hops - 1 else sent[:rows], ("tok", "proto"), along))
        if hop < hops - 1:
            crossed.append(lax.ppermute(came[-1][rows:], "proto", swap))
        if hop == 1:
            hidden, mine, _ = lax.optimization_barrier((hidden, mine, came[-1]))
            other = lax.ppermute(mine, "proto", swap)
        if hop == hops - 2:
            student_own, _ = lax.optimization_barrier((student_own, came[-1]))
    late, late_crossed = [lax.ppermute(student_own, ("tok", "proto"), along)], []
    staged = call(
        stage_kernel,
        pltpu.VMEM(hidden.shape, bf16),
        [HB],
        VM,
        (0, 16 * MIB),
        [dma((4,))],
    )(far(hidden))
    unit_teacher, full_head = call(
        neck_kernel,
        (shaped((tok_dev, width), bf16), pltpu.HBM((depth, width), bf16)),
        [SM, VM, VM, VM],
        (VM, HB),
        (2 * tok_dev * depth * width, 10 * MIB),
        [pltpu.VMEM((depth, width), bf16), pltpu.VMEM((depth, width), bf16), dma((1,))],
    )(here, held(staged), mine, other)

    blocks = came + crossed
    scores, whole_teacher, unit_kept, columns = call(
        scores_kernel,
        (
            pltpu.VMEM((tok_dev, local), bf16),
            pltpu.HBM((toks * rows, local), bf16),
            pltpu.HBM((tok_dev, width), bf16),
            shaped((toks, lines, 128), f32),
        ),
        [SM] + [VM] * (2 + len(blocks)),
        (VM, HB, HB, VM),
        (2 * tok_dev * local * width, 12 * MIB),
        [
            pltpu.VMEM((toks * rows, local), bf16),
            pltpu.VMEM((lines, 128), f32),
            dma((2,)),
        ],
    )(here, unit_teacher, both, *blocks)

    row_call = call(
        row_kernel,
        shaped((protos, tok_dev // 128, 128), bf16),
        [VM, VM],
        VM,
        (2 * tok_dev * local, 8 * MIB),
        [pltpu.VMEM((tok_dev // 128, 128), f32)],
    )
    column_call = call(
        column_kernel,
        shaped((toks, lines, 128), f32),
        [VM, VM],
        VM,
        (2 * tok_dev * local, 8 * MIB),
        [pltpu.VMEM((tok_dev, 128), f32)],
    )
    last_column_call = call(
        last_column_kernel,
        (shaped((toks, lines, 128), f32), pltpu.HBM((toks * rows, local), bf16)),
        [SM] + [VM] * (2 + 2 * hops),
        (VM, HB),
        (2 * tok_dev * local, 8 * MIB),
        [
            pltpu.VMEM((toks * rows, local), bf16),
            pltpu.VMEM((tok_dev, 128), f32),
            dma((1,)),
        ],
    )

    def onward(values):
        values, late[-1], *late_crossed[:] = lax.optimization_barrier(
            (values, late[-1], *late_crossed)
        )
        if len(late) < hops:
            late_crossed.append(lax.ppermute(late[-1][rows:], "proto", swap))
            sent = late[-1] if len(late) < hops - 1 else late[-1][:rows]
            late.append(lax.ppermute(sent, ("tok", "proto"), along))
        return values

    columns = onward(columns)
    sums = row_call(exchange(columns, "tok"), held(scores))
    sums = onward(sums)
    columns = column_call(exchange(sums, "proto"), held(scores))
    columns = onward(columns)
    sums = row_call(exchange(columns, "tok"), held(scores))
    sums = onward(sums)
    columns, whole_student = last_column_call(
        here, exchange(sums, "proto"), held(scores), both, *late, *late_crossed
    )
    columns, whole_student = lax.optimization_barrier((columns, whole_student))

    rows = toks * rows
    masked, scale_p, unit_float, grad, soft_total = call(
        student_kernel,
        (
            pltpu.VMEM((slots, local), f32),
            pltpu.HBM((8, local), f32),
            pltpu.VMEM((slots, width + 128), f32),
            pltpu.HBM((slots, width), f32),
            pltpu.HBM((slots, 128), f32),
        ),
        [VM] + [HB] * 5,
        (VM,) * 5,
        (10 * slots * local * width, 8 * MIB),
        [
            pltpu.VMEM((slots, depth), bf16),
            pltpu.VMEM((depth, width), bf16),
            pltpu.VMEM((tok_dev, width), bf16),
            pltpu.VMEM((rows, local), bf16),
            pltpu.VMEM((rows, local), bf16),
            dma((5,)),
        ],
    )(
        mask_index.reshape(1, slots),
        far(student_hidden),
        far(full_head),
        far(unit_kept),
        far(whole_teacher),
        far(whole_student),
    )

    parts = call(
        goal_kernel,
        shaped((slots, 2 * width + 128), f32),
        [VM] * 3 + [HB] * 4,
        VM,
        (4 * slots * local * width, 4 * MIB),
        [
            pltpu.VMEM((8, local), f32),
            pltpu.VMEM((rows, local), bf16),
            pltpu.VMEM((slots, 128), f32),
            dma((3 + local // 512,)),
        ],
    )(
        exchange(columns, "tok"),
        held(masked),
        held(unit_float),
        far(scale_p),
        far(whole_student),
        far(grad),
        far(soft_total),
    )
    parts = exchange(parts.reshape(protos, share, 2 * width + 128), "proto")
    finals, row_loss = call(
        slots_kernel,
        (shaped((protos, 2 * share, width // 2), bf16), shaped((slots // 128, 128), f32)),
        [SM, SM, VM, VM],
        (VM, VM),
        (2 * slots * width, MIB),
    )(here, mask_count, parts, held(unit_float))
    hidden_grad = call(
        hidden_kernel,
        shaped(student_hidden.shape, bf16),
        [VM, VM],
        VM,
        (2 * slots * width * depth, 3 * MIB),
    )(exchange(finals, "proto"), full_head)
    return (row_loss.reshape(slots), hidden_grad)


def solution(mesh):
    placed = (
        P("tok", None),
        P("proto", None),
        P("tok", "proto"),
        P("tok", None),
        P("proto", None),
        P("tok", "proto"),
        P("tok"),
        P(),
    )
    return jax.shard_map(
        shards, mesh=mesh, in_specs=placed, out_specs=(P("tok"), P("tok", None)), check_vma=False
    )
```

```python
import jax
import jax.numpy as jnp
from jax import lax
from jax.experimental import pallas as pl
from jax.experimental.pallas import tpu as pltpu
from jax.sharding import PartitionSpec as P

teacher_temp = 0.07
student_temp = 0.1
norm_eps = 1e-06
LOG2E = 1.4426950408889634
MIB = 1024 * 1024
f32 = jnp.float32
bf16 = jnp.bfloat16
VM = pl.BlockSpec(memory_space=pltpu.VMEM)
SM = pl.BlockSpec(memory_space=pltpu.SMEM)
HB = pl.BlockSpec(memory_space=pltpu.HBM)
ANY = pl.BlockSpec(memory_space=pl.ANY)
NT = (((1,), (1,)), ((), ()))


def shaped(shape, dtype):
    return jax.ShapeDtypeStruct(shape, dtype)


def call(kernel, out_shape, in_specs, out_specs, cost, scratch=(), mib=40):
    return pl.pallas_call(
        kernel,
        out_shape=out_shape,
        in_specs=in_specs,
        out_specs=out_specs,
        scratch_shapes=list(scratch),
        cost_estimate=pl.CostEstimate(flops=cost[0], bytes_accessed=cost[1], transcendentals=0),
        compiler_params=pltpu.CompilerParams(vmem_limit_bytes=mib * MIB),
    )


def held(values):
    return pltpu.with_memory_space_constraint(values, pltpu.VMEM)


def far(values):
    return pltpu.with_memory_space_constraint(values, pltpu.HBM)


def dot(left, right, dims=(((1,), (0,)), ((), ()))):
    return lax.dot_general(left, right, dims, preferred_element_type=f32)


def split(values):
    high = values.astype(bf16)
    return high, (values - high.astype(f32)).astype(bf16)


def fetch(pairs, sems, first=0):
    copies = [
        pltpu.make_async_copy(source, target, sems.at[first + k])
        for k, (source, target) in enumerate(pairs)
    ]
    for copy in copies:
        copy.start()
    return copies


def settle(copies):
    for copy in copies:
        copy.wait()


def heads_kernel(teacher, student, first, second, copies, both, v_teacher, v_student, sems):
    rows, width = first.shape[0], teacher.shape[1]
    heads = fetch([(teacher, v_teacher), (student, v_student)], sems)
    rest = fetch(
        [(first, both.at[pl.ds(0, rows), :]), (second, both.at[pl.ds(rows, rows), :])], sems, 2
    )
    settle(heads)
    copies[:, :, :width] = jnp.broadcast_to(v_teacher[...][None], copies.shape[:2] + (width,))
    copies[:, :, width:] = jnp.broadcast_to(v_student[...][None], copies.shape[:2] + (width,))
    settle(rest)


def stage_kernel(hidden, staged, sems):
    step = hidden.shape[0] // 4
    rows = [pl.ds(k * step, step) for k in range(4)]
    settle(fetch([(hidden.at[at, :], staged.at[at, :]) for at in rows], sems))


def neck_kernel(here, hidden, mine, other, unit, student, head, sems):
    chips, rows, double = mine.shape
    width = double // 2
    near, away = here[1] * rows, (1 - here[1]) * rows
    near, away = (pl.multiple_of(at, rows) for at in (near, away))
    copies = fetch(
        [
            (mine.at[:, :, width:], student.at[:, pl.ds(near, rows), :]),
            (other.at[:, :, width:], student.at[:, pl.ds(away, rows), :]),
        ],
        sems,
    )
    for chip in range(chips):
        at = 2 * rows * chip
        head[pl.ds(pl.multiple_of(at + near, rows), rows), :] = mine[chip, :, :width]
        head[pl.ds(pl.multiple_of(at + away, rows), rows), :] = other[chip, :, :width]
    step = 256
    for k in range(hidden.shape[0] // step):
        at = slice(k * step, (k + 1) * step)
        neck = dot(hidden[at, :], head[...])
        scale = lax.rsqrt(jnp.sum(neck * neck, axis=1, keepdims=True) + norm_eps)
        unit[at, :] = (neck * scale).astype(bf16)
    settle(copies)


def join_kernel(mine, other, teacher, student):
    rows = mine.shape[0] // 2
    teacher[:rows, :] = mine[:rows, :]
    teacher[rows:, :] = other[:rows, :]
    student[:rows, :] = mine[rows:, :]
    student[rows:, :] = other[rows:, :]


def place_blocks(here, own, came, crossed, whole):
    rows = own.shape[0]
    count = whole.shape[0] // rows
    way = 1 - 2 * here[1]

    def put(steps, block):
        origin = lax.rem(here[0] + way * steps + count, count) * rows
        whole[pl.ds(pl.multiple_of(origin, rows), rows), :] = block[:rows, :]

    put(0, own)
    for k, block in enumerate(came):
        put(-(k + 1), block)
    for k, block in enumerate(crossed):
        put(k + 1, block)


def scores_kernel(here, unit, own, *refs):
    blocks, refs = refs[:-7], refs[-7:]
    scores, teacher, kept, columns, whole, sums, sems = refs
    hops = (len(blocks) + 1) // 2
    place_blocks(here, own[: own.shape[0] // 2, :], blocks[:hops], blocks[hops:], whole)
    rest = fetch([(whole, teacher), (unit, kept)], sems)
    fold = LOG2E / teacher_temp
    step = 256
    count = step // 128

    def over_columns(c, _):
        at = pl.ds(pl.multiple_of(c * step, step), step)
        weights = whole[:, at]
        acc = jnp.zeros((8, step), f32)
        for r in range(unit.shape[0] // step):
            rows = slice(r * step, (r + 1) * step)
            value = jnp.exp2(dot(unit[rows, :], weights) * fold)
            scores[rows, at] = value.astype(bf16)
            acc = acc + jnp.sum(value.reshape(step // 8, 8, step), axis=0)
        acc = jnp.sum(acc, axis=0, keepdims=True)
        for k in range(count):
            sums[pl.ds(c * count + k, 1), :] = acc[:, k * 128 : (k + 1) * 128]
        return 0

    lax.fori_loop(0, whole.shape[1] // step, over_columns, 0, unroll=4)
    settle(rest)
    columns[...] = jnp.broadcast_to(sums[...][None], columns.shape)


def row_kernel(parts, scores, rows, sums):
    inverse = 1.0 / jnp.sum(parts[...], axis=0)
    group = 4

    def over_rows(i, _):
        for r in range(group):
            at = pl.ds(pl.multiple_of(i * (group * 128) + r * 128, 128), 128)
            acc = jnp.zeros((128, 128), f32)
            for c in range(scores.shape[1] // 128):
                block = scores[at, c * 128 : (c + 1) * 128].astype(f32)
                acc = acc + block * inverse[c : c + 1, :]
            sums[pl.ds(i * group + r, 1), :] = jnp.sum(acc.T, axis=0, keepdims=True)
        return 0

    lax.fori_loop(0, scores.shape[0] // (group * 128), over_rows, 0, unroll=2)
    rows[...] = jnp.broadcast_to(sums[...].astype(rows.dtype)[None], rows.shape)


def column_kernel(parts, scores, columns, weight):
    turned = (1.0 / jnp.sum(parts[...].astype(f32), axis=0)).T
    for r in range(weight.shape[0] // 128):
        weight[r * 128 : (r + 1) * 128, :] = jnp.broadcast_to(turned[:, r : r + 1], (128, 128))
    step = 64
    tiles = scores.shape[1] // 128

    def over_rows(r, acc):
        at = pl.ds(pl.multiple_of(r * step, step), step)
        w = weight[at, :]
        out = []
        for c in range(tiles):
            block = scores[at, c * 128 : (c + 1) * 128].astype(f32) * w
            out.append(acc[c] + jnp.sum(block.reshape(step // 8, 8, 128), axis=0))
        return tuple(out)

    zeros = tuple(jnp.zeros((8, 128), f32) for _ in range(tiles))
    acc = lax.fori_loop(0, scores.shape[0] // step, over_rows, zeros, unroll=8)
    total = jnp.concatenate([jnp.sum(a, axis=0, keepdims=True) for a in acc], axis=0)
    columns[...] = jnp.broadcast_to(total[None], columns.shape)


def last_column_kernel(here, parts, scores, own, *refs):
    blocks, (columns, student, whole, weight, sems) = refs[:-5], refs[-5:]
    hops = (len(blocks) + 1) // 2
    place_blocks(here, own[own.shape[0] // 2 :, :], blocks[:hops], blocks[hops:], whole)
    copies = fetch([(whole, student)], sems)
    column_kernel(parts, scores, columns, weight)
    settle(copies)


def student_kernel(index, hidden, head, unit, teacher, student, *refs):
    masked, scale_out, unit_out, grad, total = refs[:5]
    v_hidden, v_head, v_unit, v_teacher, whole, halves, sems = refs[5:]
    copies = fetch(
        [
            (hidden, v_hidden),
            (head, v_head),
            (unit, v_unit),
            (teacher, v_teacher),
            (student, whole),
        ],
        sems,
    )
    slots, tokens = v_hidden.shape[0], v_unit.shape[0]
    settle(copies[:2])
    neck = dot(v_hidden[...], v_head[...])
    scale = lax.rsqrt(jnp.sum(neck * neck, axis=1, keepdims=True) + norm_eps)
    unit_float = neck * scale
    width = v_head.shape[1]
    unit_out[:, :width] = unit_float
    unit_out[:, width:] = jnp.broadcast_to(scale, (unit_float.shape[0], 128))
    student = unit_float.astype(bf16)
    settle(copies[2:])
    wanted = jnp.broadcast_to(index[...].astype(f32), (128, slots)).T[:, 0:1]
    chosen = wanted == lax.broadcasted_iota(jnp.int32, (slots, tokens), 1).astype(f32)
    picked = dot(chosen.astype(f32).astype(bf16), v_unit[...]).astype(bf16)
    fold = LOG2E / teacher_temp
    step = 256
    total_acc = jnp.zeros((slots, 1), f32)
    for c in range(whole.shape[1] // step):
        at = slice(c * step, (c + 1) * step)
        masked[:, at] = jnp.exp2(dot(picked, v_teacher[:, at]) * fold)
        weights = whole[:, at]
        wide = weights.astype(f32)
        scale_p = lax.rsqrt(jnp.sum(wide * wide, axis=0, keepdims=True) + norm_eps) / student_temp
        scale_out[:, at] = jnp.broadcast_to(scale_p, (8, step))
        soft = jnp.exp2(dot(student, weights) * (scale_p * LOG2E))
        total_acc = total_acc + jnp.sum(soft, axis=1, keepdims=True)
        halves[:slots, at], halves[slots:, at] = split(soft * scale_p)
    both = dot(halves[...], whole[...], NT)
    grad[...] = both[:slots] + both[slots:]
    total[...] = jnp.broadcast_to(total_acc, total.shape)


def goal_kernel(
    parts, masked, unit, scale_p, whole, grad, total, out, v_scale, v_whole, v_total, halves, sems
):
    slots, width = grad.shape
    step = 512
    count = whole.shape[1] // step
    copies = fetch([(scale_p, v_scale), (total, v_total), (grad, out.at[:, :width])], sems)
    weights = fetch([(whole, v_whole)], sems, 3)
    inverse = 1.0 / jnp.sum(parts[...], axis=0)
    goal_acc = jnp.zeros((slots, 128), f32)
    settle(copies[:1])
    for c in range(count):
        pieces = []
        for k in range(c * (step // 128), (c + 1) * (step // 128)):
            at = slice(k * 128, (k + 1) * 128)
            goal = masked[:, at] * inverse[k : k + 1, :]
            goal_acc = goal_acc + goal
            pieces.append(goal * v_scale[0:1, at])
        at = slice(c * step, (c + 1) * step)
        halves[:slots, at], halves[slots:, at] = split(jnp.concatenate(pieces, axis=1))
    settle(weights)
    both = dot(halves[...], v_whole[...], NT)
    grad_acc = both[:slots] + both[slots:]
    out[:, width : 2 * width] = grad_acc
    goal_total = jnp.sum(goal_acc, axis=1, keepdims=True)
    rounded = unit[:, :width].astype(bf16).astype(f32)
    goal_dot = jnp.sum(rounded * grad_acc, axis=1, keepdims=True)
    lane = lax.broadcasted_iota(jnp.int32, (slots, 128), 1)
    settle(copies[1:])
    sums = jnp.where(lane == 0, v_total[...], jnp.where(lane == 1, goal_total, goal_dot)).T
    rows = [sums[k : k + 1, c : c + 128] for k in range(3) for c in range(0, slots, 128)]
    tile = jnp.concatenate(rows + [jnp.zeros((8 - len(rows), 128), f32)], axis=0)
    out[:, 2 * width :] = jnp.broadcast_to(tile[None], (slots // 8, 8, 128)).reshape(slots, 128)


def slots_kernel(here, counts, parts, unit_float, out, loss):
    count = counts[here[0]]
    share, width = parts.shape[1], unit_float.shape[1] - 128
    mine = jnp.sum(parts[...], axis=0)
    sums = mine[:, 2 * width :]
    slot = 128 * lax.broadcasted_iota(jnp.int32, (2, 128), 0)
    slot = slot + lax.broadcasted_iota(jnp.int32, (2, 128), 1)
    live = jnp.where(slot < count, 1.0, 0.0)
    loss[...] = live * (jnp.log(sums[0:2, :]) - sums[4:6, :] / sums[2:4, :])
    at = pl.multiple_of(here[2] * share, share)
    row = lax.div(at, 128)
    pick = lax.broadcasted_iota(jnp.int32, (share, 128), 1) == (
        lax.rem(at, 128) + lax.broadcasted_iota(jnp.int32, (share, 128), 0)
    )

    def column(first, second):
        line = jnp.where(row == 0, first, second)
        return jnp.sum(jnp.where(pick, line, 0.0), axis=1, keepdims=True)

    soft_total = column(sums[0:1, :], sums[1:2, :])
    goal_total = column(sums[2:3, :], sums[3:4, :])
    unit = unit_float[pl.ds(at, share), :width]
    scale = unit_float[pl.ds(at, share), width : width + 1]
    soft, goal = mine[:, :width] / soft_total, mine[:, width : 2 * width] / goal_total
    slot = at + lax.broadcasted_iota(jnp.int32, (share, 1), 0)
    unit_grad = jnp.where(slot < count, soft - goal, 0.0)
    inner = jnp.sum(unit * unit_grad, axis=1, keepdims=True)
    neck_grad = scale * (unit_grad - unit * inner)
    halves = jnp.concatenate([neck_grad[:, : width // 2], neck_grad[:, width // 2 :]], axis=0)
    out[...] = jnp.broadcast_to(halves.astype(bf16)[None], out.shape)


def hidden_kernel(parts, head, hidden):
    count, double, half = parts.shape
    share = double // 2
    wide = parts[...].astype(f32)
    halves = [
        wide[:, k * share : (k + 1) * share, :].reshape(count * share, half) for k in range(2)
    ]
    neck_grad = jnp.concatenate(halves, axis=1).astype(bf16)
    step = 512
    for c in range(head.shape[0] // step):
        at = slice(c * step, (c + 1) * step)
        hidden[:, at] = dot(neck_grad, head[at, :], NT).astype(bf16)


def exchange(blocks, axis, groups=None):
    return lax.all_to_all(blocks, axis, 0, 0, tiled=True, axis_index_groups=groups)


def shards(
    teacher_hidden,
    head_teacher,
    proto_teacher,
    student_hidden,
    head_student,
    proto_student,
    mask_index,
    mask_count,
):
    toks, protos = lax.axis_size("tok"), lax.axis_size("proto")
    tok, proto = lax.axis_index("tok"), lax.axis_index("proto")
    tok_dev, slots = teacher_hidden.shape[0], student_hidden.shape[0]
    depth = teacher_hidden.shape[1]
    width, local = head_teacher.shape[1], proto_teacher.shape[1]
    lines = local // 128
    share = slots // protos
    here = jnp.stack([tok, proto % 2, proto])
    dma = pltpu.SemaphoreType.DMA

    swap = [(i, i ^ 1) for i in range(protos)]
    along = []
    for t in range(toks):
        for p in range(protos):
            to = (t + (1 if p % 2 == 0 else -1)) % toks
            along.append((t * protos + p, to * protos + p))
    rows = proto_teacher.shape[0]

    chips = protos // 2
    groups = [[2 * k + c for k in range(chips)] for c in range(2)]
    copies, both = call(
        heads_kernel,
        (shaped((chips, depth // protos, 2 * width), bf16), shaped((2 * rows, local), bf16)),
        [HB] * 4,
        (VM, VM),
        (0, MIB),
        [pltpu.VMEM((depth // protos, width), bf16)] * 2 + [dma((4,))],
    )(far(head_teacher), far(head_student), far(proto_teacher), far(proto_student))
    mine = exchange(copies, "proto", groups)
    sibling = lax.ppermute(both, "proto", swap)
    chains = call(
        join_kernel,
        (shaped((2 * rows, local), bf16),) * 2,
        [VM, VM],
        (VM, VM),
        (0, MIB),
    )(both, sibling)
    teacher_own, student_own = chains
    hops = toks // 2
    hidden = teacher_hidden
    came, crossed = [], []
    for hop in range(hops):
        sent = came[-1] if hop else teacher_own
        came.append(lax.ppermute(sent if hop < hops - 1 else sent[:rows], ("tok", "proto"), along))
        if hop < hops - 1:
            crossed.append(lax.ppermute(came[-1][rows:], "proto", swap))
        if hop == 1:
            hidden, mine, _ = lax.optimization_barrier((hidden, mine, came[-1]))
            other = lax.ppermute(mine, "proto", swap)
        if hop == hops - 2:
            student_own, _ = lax.optimization_barrier((student_own, came[-1]))
    late, late_crossed = [lax.ppermute(student_own, ("tok", "proto"), along)], []
    staged = call(
        stage_kernel,
        pltpu.VMEM(hidden.shape, bf16),
        [HB],
        VM,
        (0, 16 * MIB),
        [dma((4,))],
    )(far(hidden))
    unit_teacher, full_head = call(
        neck_kernel,
        (
            shaped((tok_dev, width), bf16),
            pltpu.HBM((chips, depth // chips, width), bf16),
        ),
        [SM, VM, VM, VM],
        (VM, HB),
        (2 * tok_dev * depth * width, 10 * MIB),
        [pltpu.VMEM((depth, width), bf16), dma((2,))],
    )(here, held(staged), mine, other)
    full_head = full_head.reshape(depth, width)

    blocks = came + crossed
    scores, whole_teacher, unit_kept, columns = call(
        scores_kernel,
        (
            pltpu.VMEM((tok_dev, local), bf16),
            pltpu.HBM((toks * rows, local), bf16),
            pltpu.HBM((tok_dev, width), bf16),
            shaped((toks, lines, 128), f32),
        ),
        [SM] + [VM] * (2 + len(blocks)),
        (VM, HB, HB, VM),
        (2 * tok_dev * local * width, 12 * MIB),
        [
            pltpu.VMEM((toks * rows, local), bf16),
            pltpu.VMEM((lines, 128), f32),
            dma((2,)),
        ],
    )(here, unit_teacher, both, *blocks)

    row_call = call(
        row_kernel,
        shaped((protos, tok_dev // 128, 128), bf16),
        [VM, VM],
        VM,
        (2 * tok_dev * local, 8 * MIB),
        [pltpu.VMEM((tok_dev // 128, 128), f32)],
    )
    column_call = call(
        column_kernel,
        shaped((toks, lines, 128), f32),
        [VM, VM],
        VM,
        (2 * tok_dev * local, 8 * MIB),
        [pltpu.VMEM((tok_dev, 128), f32)],
    )
    last_column_call = call(
        last_column_kernel,
        (shaped((toks, lines, 128), f32), pltpu.HBM((toks * rows, local), bf16)),
        [SM] + [VM] * (2 + 2 * hops),
        (VM, HB),
        (2 * tok_dev * local, 8 * MIB),
        [
            pltpu.VMEM((toks * rows, local), bf16),
            pltpu.VMEM((tok_dev, 128), f32),
            dma((1,)),
        ],
    )

    def onward(values):
        values, late[-1], *late_crossed[:] = lax.optimization_barrier(
            (values, late[-1], *late_crossed)
        )
        if len(late) < hops:
            late_crossed.append(lax.ppermute(late[-1][rows:], "proto", swap))
            sent = late[-1] if len(late) < hops - 1 else late[-1][:rows]
            late.append(lax.ppermute(sent, ("tok", "proto"), along))
        return values

    columns = onward(columns)
    sums = row_call(exchange(columns, "tok"), held(scores))
    sums = onward(sums)
    columns = column_call(exchange(sums, "proto"), held(scores))
    columns = onward(columns)
    sums = row_call(exchange(columns, "tok"), held(scores))
    sums = onward(sums)
    columns, whole_student = last_column_call(
        here, exchange(sums, "proto"), held(scores), both, *late, *late_crossed
    )
    columns, whole_student = lax.optimization_barrier((columns, whole_student))

    rows = toks * rows
    masked, scale_p, unit_float, grad, soft_total = call(
        student_kernel,
        (
            pltpu.VMEM((slots, local), f32),
            pltpu.HBM((8, local), f32),
            pltpu.VMEM((slots, width + 128), f32),
            pltpu.HBM((slots, width), f32),
            pltpu.HBM((slots, 128), f32),
        ),
        [VM] + [HB] * 5,
        (VM,) * 5,
        (10 * slots * local * width, 8 * MIB),
        [
            pltpu.VMEM((slots, depth), bf16),
            pltpu.VMEM((depth, width), bf16),
            pltpu.VMEM((tok_dev, width), bf16),
            pltpu.VMEM((rows, local), bf16),
            pltpu.VMEM((rows, local), bf16),
            pltpu.VMEM((2 * slots, local), bf16),
            dma((5,)),
        ],
    )(
        mask_index.reshape(1, slots),
        far(student_hidden),
        far(full_head),
        far(unit_kept),
        far(whole_teacher),
        far(whole_student),
    )

    parts = call(
        goal_kernel,
        shaped((slots, 2 * width + 128), f32),
        [VM] * 3 + [HB] * 4,
        VM,
        (4 * slots * local * width, 4 * MIB),
        [
            pltpu.VMEM((8, local), f32),
            pltpu.VMEM((rows, local), bf16),
            pltpu.VMEM((slots, 128), f32),
            pltpu.VMEM((2 * slots, local), bf16),
            dma((4,)),
        ],
    )(
        exchange(columns, "tok"),
        held(masked),
        held(unit_float),
        far(scale_p),
        far(whole_student),
        far(grad),
        far(soft_total),
    )
    parts = exchange(parts.reshape(protos, share, 2 * width + 128), "proto")
    finals, row_loss = call(
        slots_kernel,
        (shaped((protos, 2 * share, width // 2), bf16), shaped((slots // 128, 128), f32)),
        [SM, SM, VM, VM],
        (VM, VM),
        (2 * slots * width, MIB),
    )(here, mask_count, parts, held(unit_float))
    hidden_grad = call(
        hidden_kernel,
        shaped(student_hidden.shape, bf16),
        [VM, VM],
        VM,
        (2 * slots * width * depth, 3 * MIB),
    )(exchange(finals, "proto"), full_head)
    return (row_loss.reshape(slots), hidden_grad)


def solution(mesh):
    placed = (
        P("tok", None),
        P("proto", None),
        P("tok", "proto"),
        P("tok", None),
        P("proto", None),
        P("tok", "proto"),
        P("tok"),
        P(),
    )
    return jax.shard_map(
        shards, mesh=mesh, in_specs=placed, out_specs=(P("tok"), P("tok", None)), check_vma=False
    )
```

```python
import jax
import jax.numpy as jnp
from jax import lax
from jax.experimental import pallas as pl
from jax.experimental.pallas import tpu as pltpu
from jax.sharding import PartitionSpec as P

teacher_temp = 0.07
student_temp = 0.1
norm_eps = 1e-06
LOG2E = 1.4426950408889634
MIB = 1024 * 1024
f32 = jnp.float32
bf16 = jnp.bfloat16
VM = pl.BlockSpec(memory_space=pltpu.VMEM)
SM = pl.BlockSpec(memory_space=pltpu.SMEM)
HB = pl.BlockSpec(memory_space=pltpu.HBM)
ANY = pl.BlockSpec(memory_space=pl.ANY)
NT = (((1,), (1,)), ((), ()))


def shaped(shape, dtype):
    return jax.ShapeDtypeStruct(shape, dtype)


def call(kernel, out_shape, in_specs, out_specs, cost, scratch=(), mib=40):
    return pl.pallas_call(
        kernel,
        out_shape=out_shape,
        in_specs=in_specs,
        out_specs=out_specs,
        scratch_shapes=list(scratch),
        cost_estimate=pl.CostEstimate(flops=cost[0], bytes_accessed=cost[1], transcendentals=0),
        compiler_params=pltpu.CompilerParams(vmem_limit_bytes=mib * MIB),
    )


def held(values):
    return pltpu.with_memory_space_constraint(values, pltpu.VMEM)


def far(values):
    return pltpu.with_memory_space_constraint(values, pltpu.HBM)


def dot(left, right, dims=(((1,), (0,)), ((), ()))):
    return lax.dot_general(left, right, dims, preferred_element_type=f32)


def split(values):
    high = values.astype(bf16)
    return high, (values - high.astype(f32)).astype(bf16)


def fetch(pairs, sems, first=0):
    copies = [
        pltpu.make_async_copy(source, target, sems.at[first + k])
        for k, (source, target) in enumerate(pairs)
    ]
    for copy in copies:
        copy.start()
    return copies


def settle(copies):
    for copy in copies:
        copy.wait()


def heads_kernel(teacher, student, first, second, copies, both, v_teacher, v_student, sems):
    rows, width = first.shape[0], teacher.shape[1]
    heads = fetch([(teacher, v_teacher), (student, v_student)], sems)
    rest = fetch(
        [(first, both.at[pl.ds(0, rows), :]), (second, both.at[pl.ds(rows, rows), :])], sems, 2
    )
    settle(heads)
    copies[:, :, :width] = jnp.broadcast_to(v_teacher[...][None], copies.shape[:2] + (width,))
    copies[:, :, width:] = jnp.broadcast_to(v_student[...][None], copies.shape[:2] + (width,))
    settle(rest)


def stage_kernel(hidden, staged, sems):
    step = hidden.shape[0] // 4
    rows = [pl.ds(k * step, step) for k in range(4)]
    settle(fetch([(hidden.at[at, :], staged.at[at, :]) for at in rows], sems))


def neck_kernel(here, hidden, mine, other, unit, student, head, sems):
    chips, rows, double = mine.shape
    width = double // 2
    near, away = here[1] * rows, (1 - here[1]) * rows
    near, away = (pl.multiple_of(at, rows) for at in (near, away))
    copies = fetch(
        [
            (mine.at[:, :, width:], student.at[:, pl.ds(near, rows), :]),
            (other.at[:, :, width:], student.at[:, pl.ds(away, rows), :]),
        ],
        sems,
    )
    for chip in range(chips):
        at = 2 * rows * chip
        head[pl.ds(pl.multiple_of(at + near, rows), rows), :] = mine[chip, :, :width]
        head[pl.ds(pl.multiple_of(at + away, rows), rows), :] = other[chip, :, :width]
    step = 256
    for k in range(hidden.shape[0] // step):
        at = slice(k * step, (k + 1) * step)
        neck = dot(hidden[at, :], head[...])
        scale = lax.rsqrt(jnp.sum(neck * neck, axis=1, keepdims=True) + norm_eps)
        unit[at, :] = (neck * scale).astype(bf16)
    settle(copies)


def join_kernel(mine, other, teacher, student):
    rows = mine.shape[0] // 2
    teacher[:rows, :] = mine[:rows, :]
    teacher[rows:, :] = other[:rows, :]
    student[:rows, :] = mine[rows:, :]
    student[rows:, :] = other[rows:, :]


def place_blocks(here, own, came, crossed, whole):
    rows = own.shape[0]
    count = whole.shape[0] // rows
    way = 1 - 2 * here[1]

    def put(steps, block):
        origin = lax.rem(here[0] + way * steps + count, count) * rows
        whole[pl.ds(pl.multiple_of(origin, rows), rows), :] = block[:rows, :]

    put(0, own)
    for k, block in enumerate(came):
        put(-(k + 1), block)
    for k, block in enumerate(crossed):
        put(k + 1, block)


def scores_kernel(here, unit, own, *refs):
    blocks, refs = refs[:-7], refs[-7:]
    scores, teacher, kept, columns, whole, sums, sems = refs
    hops = (len(blocks) + 1) // 2
    place_blocks(here, own[: own.shape[0] // 2, :], blocks[:hops], blocks[hops:], whole)
    rest = fetch([(whole, teacher), (unit, kept)], sems)
    fold = LOG2E / teacher_temp
    step = 256
    count = step // 128

    def over_columns(c, _):
        at = pl.ds(pl.multiple_of(c * step, step), step)
        weights = whole[:, at]
        acc = jnp.zeros((8, step), f32)
        for r in range(unit.shape[0] // step):
            rows = slice(r * step, (r + 1) * step)
            value = jnp.exp2(dot(unit[rows, :], weights) * fold)
            scores[rows, at] = value.astype(bf16)
            acc = acc + jnp.sum(value.reshape(step // 8, 8, step), axis=0)
        acc = jnp.sum(acc, axis=0, keepdims=True)
        for k in range(count):
            sums[pl.ds(c * count + k, 1), :] = acc[:, k * 128 : (k + 1) * 128]
        return 0

    lax.fori_loop(0, whole.shape[1] // step, over_columns, 0, unroll=4)
    settle(rest)
    columns[...] = jnp.broadcast_to(sums[...][None], columns.shape)


def row_kernel(parts, scores, rows, sums):
    inverse = 1.0 / jnp.sum(parts[...], axis=0)
    group = 4

    def over_rows(i, _):
        for r in range(group):
            at = pl.ds(pl.multiple_of(i * (group * 128) + r * 128, 128), 128)
            acc = jnp.zeros((128, 128), f32)
            for c in range(scores.shape[1] // 128):
                block = scores[at, c * 128 : (c + 1) * 128].astype(f32)
                acc = acc + block * inverse[c : c + 1, :]
            sums[pl.ds(i * group + r, 1), :] = jnp.sum(acc.T, axis=0, keepdims=True)
        return 0

    lax.fori_loop(0, scores.shape[0] // (group * 128), over_rows, 0, unroll=2)
    rows[...] = jnp.broadcast_to(sums[...].astype(rows.dtype)[None], rows.shape)


def column_kernel(parts, scores, columns, weight):
    turned = (1.0 / jnp.sum(parts[...].astype(f32), axis=0)).T
    for r in range(weight.shape[0] // 128):
        weight[r * 128 : (r + 1) * 128, :] = jnp.broadcast_to(turned[:, r : r + 1], (128, 128))
    step = 64
    tiles = scores.shape[1] // 128

    def over_rows(r, acc):
        at = pl.ds(pl.multiple_of(r * step, step), step)
        w = weight[at, :]
        out = []
        for c in range(tiles):
            block = scores[at, c * 128 : (c + 1) * 128].astype(f32) * w
            out.append(acc[c] + jnp.sum(block.reshape(step // 8, 8, 128), axis=0))
        return tuple(out)

    zeros = tuple(jnp.zeros((8, 128), f32) for _ in range(tiles))
    acc = lax.fori_loop(0, scores.shape[0] // step, over_rows, zeros, unroll=8)
    total = jnp.concatenate([jnp.sum(a, axis=0, keepdims=True) for a in acc], axis=0)
    columns[...] = jnp.broadcast_to(total[None], columns.shape)


def last_column_kernel(here, parts, scores, own, *refs):
    blocks, (columns, student, whole, weight, sems) = refs[:-5], refs[-5:]
    hops = (len(blocks) + 1) // 2
    place_blocks(here, own[own.shape[0] // 2 :, :], blocks[:hops], blocks[hops:], whole)
    copies = fetch([(whole, student)], sems)
    column_kernel(parts, scores, columns, weight)
    settle(copies)


def student_kernel(index, hidden, head, unit, teacher, student, *refs):
    masked, scale_out, unit_out, grad, total = refs[:5]
    v_hidden, v_head, v_unit, v_teacher, whole, halves, sems = refs[5:]
    copies = fetch(
        [
            (hidden, v_hidden),
            (head, v_head),
            (unit, v_unit),
            (teacher, v_teacher),
            (student, whole),
        ],
        sems,
    )
    slots, tokens = v_hidden.shape[0], v_unit.shape[0]
    settle(copies[:2])
    neck = dot(v_hidden[...], v_head[...])
    scale = lax.rsqrt(jnp.sum(neck * neck, axis=1, keepdims=True) + norm_eps)
    unit_float = neck * scale
    width = v_head.shape[1]
    unit_out[:, :width] = unit_float
    unit_out[:, width:] = jnp.broadcast_to(scale, (unit_float.shape[0], 128))
    student = unit_float.astype(bf16)
    settle(copies[2:])
    wanted = jnp.broadcast_to(index[...].astype(f32), (128, slots)).T[:, 0:1]
    chosen = wanted == lax.broadcasted_iota(jnp.int32, (slots, tokens), 1).astype(f32)
    picked = dot(chosen.astype(f32).astype(bf16), v_unit[...]).astype(bf16)
    fold = LOG2E / teacher_temp
    step = 256
    total_acc = jnp.zeros((slots, 1), f32)
    for c in range(whole.shape[1] // step):
        at = slice(c * step, (c + 1) * step)
        masked[:, at] = jnp.exp2(dot(picked, v_teacher[:, at]) * fold)
        weights = whole[:, at]
        wide = weights.astype(f32)
        scale_p = lax.rsqrt(jnp.sum(wide * wide, axis=0, keepdims=True) + norm_eps) / student_temp
        scale_out[:, at] = jnp.broadcast_to(scale_p, (8, step))
        soft = jnp.exp2(dot(student, weights) * (scale_p * LOG2E))
        total_acc = total_acc + jnp.sum(soft, axis=1, keepdims=True)
        halves[:slots, at], halves[slots:, at] = split(soft * scale_p)
    both = dot(halves[...], whole[...], NT)
    grad[...] = both[:slots] + both[slots:]
    total[...] = jnp.broadcast_to(total_acc, total.shape)


def goal_kernel(
    here,
    parts,
    masked,
    unit,
    scale_p,
    whole,
    grad,
    total,
    keep,
    give,
    out,
    v_scale,
    v_whole,
    v_total,
    halves,
    sems,
):
    slots, width = grad.shape
    step = 512
    count = whole.shape[1] // step
    copies = fetch([(scale_p, v_scale), (total, v_total), (grad, out.at[:, :width])], sems)
    weights = fetch([(whole, v_whole)], sems, 3)
    inverse = 1.0 / jnp.sum(parts[...], axis=0)
    goal_acc = jnp.zeros((slots, 128), f32)
    settle(copies[:1])
    for c in range(count):
        pieces = []
        for k in range(c * (step // 128), (c + 1) * (step // 128)):
            at = slice(k * 128, (k + 1) * 128)
            goal = masked[:, at] * inverse[k : k + 1, :]
            goal_acc = goal_acc + goal
            pieces.append(goal * v_scale[0:1, at])
        at = slice(c * step, (c + 1) * step)
        halves[:slots, at], halves[slots:, at] = split(jnp.concatenate(pieces, axis=1))
    settle(weights)
    both = dot(halves[...], v_whole[...], NT)
    grad_acc = both[:slots] + both[slots:]
    out[:, width : 2 * width] = grad_acc
    goal_total = jnp.sum(goal_acc, axis=1, keepdims=True)
    rounded = unit[:, :width].astype(bf16).astype(f32)
    goal_dot = jnp.sum(rounded * grad_acc, axis=1, keepdims=True)
    lane = lax.broadcasted_iota(jnp.int32, (slots, 128), 1)
    settle(copies[1:])
    sums = jnp.where(lane == 0, v_total[...], jnp.where(lane == 1, goal_total, goal_dot)).T
    rows = [sums[k : k + 1, c : c + 128] for k in range(3) for c in range(0, slots, 128)]
    tile = jnp.concatenate(rows + [jnp.zeros((8 - len(rows), 128), f32)], axis=0)
    out[:, 2 * width :] = jnp.broadcast_to(tile[None], (slots // 8, 8, 128)).reshape(slots, 128)
    half = slots // 2
    keep[...] = out[pl.ds(pl.multiple_of(here[1] * half, half), half), :]
    give[...] = out[pl.ds(pl.multiple_of((1 - here[1]) * half, half), half), :]


def add_kernel(first, second, out):
    out[...] = first[...] + second[...]


def slots_kernel(here, counts, parts, unit_float, out, loss):
    count = counts[here[0]]
    share, width = parts.shape[1], unit_float.shape[1] - 128
    mine = jnp.sum(parts[...], axis=0)
    sums = mine[:, 2 * width :]
    slot = 128 * lax.broadcasted_iota(jnp.int32, (2, 128), 0)
    slot = slot + lax.broadcasted_iota(jnp.int32, (2, 128), 1)
    live = jnp.where(slot < count, 1.0, 0.0)
    loss[...] = live * (jnp.log(sums[0:2, :]) - sums[4:6, :] / sums[2:4, :])
    at = here[1] * (unit_float.shape[0] // 2) + lax.div(here[2], 2) * share
    at = pl.multiple_of(at, share)
    row = lax.div(at, 128)
    pick = lax.broadcasted_iota(jnp.int32, (share, 128), 1) == (
        lax.rem(at, 128) + lax.broadcasted_iota(jnp.int32, (share, 128), 0)
    )

    def column(first, second):
        line = jnp.where(row == 0, first, second)
        return jnp.sum(jnp.where(pick, line, 0.0), axis=1, keepdims=True)

    soft_total = column(sums[0:1, :], sums[1:2, :])
    goal_total = column(sums[2:3, :], sums[3:4, :])
    unit = unit_float[pl.ds(at, share), :width]
    scale = unit_float[pl.ds(at, share), width : width + 1]
    soft, goal = mine[:, :width] / soft_total, mine[:, width : 2 * width] / goal_total
    slot = at + lax.broadcasted_iota(jnp.int32, (share, 1), 0)
    unit_grad = jnp.where(slot < count, soft - goal, 0.0)
    inner = jnp.sum(unit * unit_grad, axis=1, keepdims=True)
    neck_grad = scale * (unit_grad - unit * inner)
    halves = jnp.concatenate([neck_grad[:, : width // 2], neck_grad[:, width // 2 :]], axis=0)
    out[...] = jnp.broadcast_to(halves.astype(bf16)[None], out.shape)


def hidden_kernel(parts, head, hidden):
    count, double, half = parts.shape
    share = double // 2
    wide = parts[...].astype(f32).reshape(count // 2, 2, double, half)
    halves = []
    for k in range(2):
        rows = [wide[:, c, k * share : (k + 1) * share, :] for c in range(2)]
        rows = [part.reshape(count // 2 * share, half) for part in rows]
        halves.append(jnp.concatenate(rows, axis=0))
    neck_grad = jnp.concatenate(halves, axis=1).astype(bf16)
    step = 512
    for c in range(head.shape[0] // step):
        at = slice(c * step, (c + 1) * step)
        hidden[:, at] = dot(neck_grad, head[at, :], NT).astype(bf16)


def exchange(blocks, axis, groups=None):
    return lax.all_to_all(blocks, axis, 0, 0, tiled=True, axis_index_groups=groups)


def shards(
    teacher_hidden,
    head_teacher,
    proto_teacher,
    student_hidden,
    head_student,
    proto_student,
    mask_index,
    mask_count,
):
    toks, protos = lax.axis_size("tok"), lax.axis_size("proto")
    tok, proto = lax.axis_index("tok"), lax.axis_index("proto")
    tok_dev, slots = teacher_hidden.shape[0], student_hidden.shape[0]
    depth = teacher_hidden.shape[1]
    width, local = head_teacher.shape[1], proto_teacher.shape[1]
    lines = local // 128
    share = slots // protos
    here = jnp.stack([tok, proto % 2, proto])
    dma = pltpu.SemaphoreType.DMA

    swap = [(i, i ^ 1) for i in range(protos)]
    along = []
    for t in range(toks):
        for p in range(protos):
            to = (t + (1 if p % 2 == 0 else -1)) % toks
            along.append((t * protos + p, to * protos + p))
    rows = proto_teacher.shape[0]

    chips = protos // 2
    groups = [[2 * k + c for k in range(chips)] for c in range(2)]
    copies, both = call(
        heads_kernel,
        (shaped((chips, depth // protos, 2 * width), bf16), shaped((2 * rows, local), bf16)),
        [HB] * 4,
        (VM, VM),
        (0, MIB),
        [pltpu.VMEM((depth // protos, width), bf16)] * 2 + [dma((4,))],
    )(far(head_teacher), far(head_student), far(proto_teacher), far(proto_student))
    mine = exchange(copies, "proto", groups)
    sibling = lax.ppermute(both, "proto", swap)
    chains = call(
        join_kernel,
        (shaped((2 * rows, local), bf16),) * 2,
        [VM, VM],
        (VM, VM),
        (0, MIB),
    )(both, sibling)
    teacher_own, student_own = chains
    hops = toks // 2
    hidden = teacher_hidden
    came, crossed = [], []
    for hop in range(hops):
        sent = came[-1] if hop else teacher_own
        came.append(lax.ppermute(sent if hop < hops - 1 else sent[:rows], ("tok", "proto"), along))
        if hop < hops - 1:
            crossed.append(lax.ppermute(came[-1][rows:], "proto", swap))
        if hop == 1:
            hidden, mine, _ = lax.optimization_barrier((hidden, mine, came[-1]))
            other = lax.ppermute(mine, "proto", swap)
        if hop == hops - 2:
            student_own, _ = lax.optimization_barrier((student_own, came[-1]))
    late, late_crossed = [lax.ppermute(student_own, ("tok", "proto"), along)], []
    staged = call(
        stage_kernel,
        pltpu.VMEM(hidden.shape, bf16),
        [HB],
        VM,
        (0, 16 * MIB),
        [dma((4,))],
    )(far(hidden))
    unit_teacher, full_head = call(
        neck_kernel,
        (
            shaped((tok_dev, width), bf16),
            pltpu.HBM((chips, depth // chips, width), bf16),
        ),
        [SM, VM, VM, VM],
        (VM, HB),
        (2 * tok_dev * depth * width, 10 * MIB),
        [pltpu.VMEM((depth, width), bf16), dma((2,))],
    )(here, held(staged), mine, other)
    full_head = full_head.reshape(depth, width)

    blocks = came + crossed
    scores, whole_teacher, unit_kept, columns = call(
        scores_kernel,
        (
            pltpu.VMEM((tok_dev, local), bf16),
            pltpu.HBM((toks * rows, local), bf16),
            pltpu.HBM((tok_dev, width), bf16),
            shaped((toks, lines, 128), f32),
        ),
        [SM] + [VM] * (2 + len(blocks)),
        (VM, HB, HB, VM),
        (2 * tok_dev * local * width, 12 * MIB),
        [
            pltpu.VMEM((toks * rows, local), bf16),
            pltpu.VMEM((lines, 128), f32),
            dma((2,)),
        ],
    )(here, unit_teacher, both, *blocks)

    row_call = call(
        row_kernel,
        shaped((protos, tok_dev // 128, 128), bf16),
        [VM, VM],
        VM,
        (2 * tok_dev * local, 8 * MIB),
        [pltpu.VMEM((tok_dev // 128, 128), f32)],
    )
    column_call = call(
        column_kernel,
        shaped((toks, lines, 128), f32),
        [VM, VM],
        VM,
        (2 * tok_dev * local, 8 * MIB),
        [pltpu.VMEM((tok_dev, 128), f32)],
    )
    last_column_call = call(
        last_column_kernel,
        (shaped((toks, lines, 128), f32), pltpu.HBM((toks * rows, local), bf16)),
        [SM] + [VM] * (2 + 2 * hops),
        (VM, HB),
        (2 * tok_dev * local, 8 * MIB),
        [
            pltpu.VMEM((toks * rows, local), bf16),
            pltpu.VMEM((tok_dev, 128), f32),
            dma((1,)),
        ],
    )

    def onward(values):
        values, late[-1], *late_crossed[:] = lax.optimization_barrier(
            (values, late[-1], *late_crossed)
        )
        if len(late) < hops:
            late_crossed.append(lax.ppermute(late[-1][rows:], "proto", swap))
            sent = late[-1] if len(late) < hops - 1 else late[-1][:rows]
            late.append(lax.ppermute(sent, ("tok", "proto"), along))
        return values

    columns = onward(columns)
    sums = row_call(exchange(columns, "tok"), held(scores))
    sums = onward(sums)
    columns = column_call(exchange(sums, "proto"), held(scores))
    columns = onward(columns)
    sums = row_call(exchange(columns, "tok"), held(scores))
    sums = onward(sums)
    columns, whole_student = last_column_call(
        here, exchange(sums, "proto"), held(scores), both, *late, *late_crossed
    )
    columns, whole_student = lax.optimization_barrier((columns, whole_student))

    rows = toks * rows
    masked, scale_p, unit_float, grad, soft_total = call(
        student_kernel,
        (
            pltpu.VMEM((slots, local), f32),
            pltpu.HBM((8, local), f32),
            pltpu.VMEM((slots, width + 128), f32),
            pltpu.HBM((slots, width), f32),
            pltpu.HBM((slots, 128), f32),
        ),
        [VM] + [HB] * 5,
        (VM,) * 5,
        (10 * slots * local * width, 8 * MIB),
        [
            pltpu.VMEM((slots, depth), bf16),
            pltpu.VMEM((depth, width), bf16),
            pltpu.VMEM((tok_dev, width), bf16),
            pltpu.VMEM((rows, local), bf16),
            pltpu.VMEM((rows, local), bf16),
            pltpu.VMEM((2 * slots, local), bf16),
            dma((5,)),
        ],
    )(
        mask_index.reshape(1, slots),
        far(student_hidden),
        far(full_head),
        far(unit_kept),
        far(whole_teacher),
        far(whole_student),
    )

    lanes = 2 * width + 128
    keep, give = call(
        goal_kernel,
        (shaped((slots // 2, lanes), f32),) * 2,
        [SM] + [VM] * 3 + [HB] * 4,
        (VM, VM),
        (4 * slots * local * width, 4 * MIB),
        [
            pltpu.VMEM((slots, lanes), f32),
            pltpu.VMEM((8, local), f32),
            pltpu.VMEM((rows, local), bf16),
            pltpu.VMEM((slots, 128), f32),
            pltpu.VMEM((2 * slots, local), bf16),
            dma((4,)),
        ],
    )(
        here,
        exchange(columns, "tok"),
        held(masked),
        held(unit_float),
        far(scale_p),
        far(whole_student),
        far(grad),
        far(soft_total),
    )
    parts = call(add_kernel, shaped((slots // 2, lanes), f32), [VM, VM], VM, (0, MIB))(
        keep, lax.ppermute(give, "proto", swap)
    )
    parts = exchange(parts.reshape(chips, share, lanes), "proto", groups)
    finals, row_loss = call(
        slots_kernel,
        (shaped((protos, 2 * share, width // 2), bf16), shaped((slots // 128, 128), f32)),
        [SM, SM, VM, VM],
        (VM, VM),
        (2 * slots * width, MIB),
    )(here, mask_count, parts, held(unit_float))
    hidden_grad = call(
        hidden_kernel,
        shaped(student_hidden.shape, bf16),
        [VM, VM],
        VM,
        (2 * slots * width * depth, 3 * MIB),
    )(exchange(finals, "proto"), full_head)
    return (row_loss.reshape(slots), hidden_grad)


def solution(mesh):
    placed = (
        P("tok", None),
        P("proto", None),
        P("tok", "proto"),
        P("tok", None),
        P("proto", None),
        P("tok", "proto"),
        P("tok"),
        P(),
    )
    return jax.shard_map(
        shards, mesh=mesh, in_specs=placed, out_specs=(P("tok"), P("tok", None)), check_vma=False
    )
```

```python
import jax
import jax.numpy as jnp
from jax import lax
from jax.experimental import pallas as pl
from jax.experimental.pallas import tpu as pltpu
from jax.sharding import PartitionSpec as P

teacher_temp = 0.07
student_temp = 0.1
norm_eps = 1e-06
LOG2E = 1.4426950408889634
MIB = 1024 * 1024
f32 = jnp.float32
bf16 = jnp.bfloat16
VM = pl.BlockSpec(memory_space=pltpu.VMEM)
SM = pl.BlockSpec(memory_space=pltpu.SMEM)
HB = pl.BlockSpec(memory_space=pltpu.HBM)
ANY = pl.BlockSpec(memory_space=pl.ANY)
NT = (((1,), (1,)), ((), ()))


def shaped(shape, dtype):
    return jax.ShapeDtypeStruct(shape, dtype)


def call(kernel, out_shape, in_specs, out_specs, cost, scratch=(), mib=40):
    return pl.pallas_call(
        kernel,
        out_shape=out_shape,
        in_specs=in_specs,
        out_specs=out_specs,
        scratch_shapes=list(scratch),
        cost_estimate=pl.CostEstimate(flops=cost[0], bytes_accessed=cost[1], transcendentals=0),
        compiler_params=pltpu.CompilerParams(vmem_limit_bytes=mib * MIB),
    )


def held(values):
    return pltpu.with_memory_space_constraint(values, pltpu.VMEM)


def far(values):
    return pltpu.with_memory_space_constraint(values, pltpu.HBM)


def dot(left, right, dims=(((1,), (0,)), ((), ()))):
    return lax.dot_general(left, right, dims, preferred_element_type=f32)


def split(values):
    high = values.astype(bf16)
    return high, (values - high.astype(f32)).astype(bf16)


def fetch(pairs, sems, first=0):
    copies = [
        pltpu.make_async_copy(source, target, sems.at[first + k])
        for k, (source, target) in enumerate(pairs)
    ]
    for copy in copies:
        copy.start()
    return copies


def settle(copies):
    for copy in copies:
        copy.wait()


def heads_kernel(teacher, student, first, second, copies, both, v_heads, sems):
    rows, width = first.shape[0], teacher.shape[1]
    heads = fetch([(teacher, v_heads.at[:, :width]), (student, v_heads.at[:, width:])], sems)
    rest = fetch(
        [(first, both.at[pl.ds(0, rows), :]), (second, both.at[pl.ds(rows, rows), :])], sems, 2
    )
    settle(heads)
    rest += fetch([(v_heads, copies.at[k]) for k in range(copies.shape[0])], sems, 4)
    settle(rest)


def stage_kernel(hidden, staged, sems):
    step = hidden.shape[0] // 4
    rows = [pl.ds(k * step, step) for k in range(4)]
    settle(fetch([(hidden.at[at, :], staged.at[at, :]) for at in rows], sems))


def neck_kernel(here, hidden, mine, other, unit, student, head, sems):
    chips, rows, double = mine.shape
    width = double // 2
    near, away = here[1] * rows, (1 - here[1]) * rows
    near, away = (pl.multiple_of(at, rows) for at in (near, away))
    copies = fetch(
        [
            (mine.at[:, :, width:], student.at[:, pl.ds(near, rows), :]),
            (other.at[:, :, width:], student.at[:, pl.ds(away, rows), :]),
        ],
        sems,
    )
    for chip in range(chips):
        at = 2 * rows * chip
        head[pl.ds(pl.multiple_of(at + near, rows), rows), :] = mine[chip, :, :width]
        head[pl.ds(pl.multiple_of(at + away, rows), rows), :] = other[chip, :, :width]
    step = 256
    for k in range(hidden.shape[0] // step):
        at = slice(k * step, (k + 1) * step)
        neck = dot(hidden[at, :], head[...])
        scale = lax.rsqrt(jnp.sum(neck * neck, axis=1, keepdims=True) + norm_eps)
        unit[at, :] = (neck * scale).astype(bf16)
    settle(copies)


def join_kernel(mine, other, teacher, student):
    rows = mine.shape[0] // 2
    teacher[:rows, :] = mine[:rows, :]
    teacher[rows:, :] = other[:rows, :]
    student[:rows, :] = mine[rows:, :]
    student[rows:, :] = other[rows:, :]


def place_blocks(here, own, came, crossed, whole):
    rows = own.shape[0]
    count = whole.shape[0] // rows
    way = 1 - 2 * here[1]

    def put(steps, block):
        origin = lax.rem(here[0] + way * steps + count, count) * rows
        whole[pl.ds(pl.multiple_of(origin, rows), rows), :] = block[:rows, :]

    put(0, own)
    for k, block in enumerate(came):
        put(-(k + 1), block)
    for k, block in enumerate(crossed):
        put(k + 1, block)


def scores_kernel(here, unit, own, *refs):
    blocks, refs = refs[:-7], refs[-7:]
    scores, teacher, kept, columns, whole, sums, sems = refs
    hops = (len(blocks) + 1) // 2
    place_blocks(here, own[: own.shape[0] // 2, :], blocks[:hops], blocks[hops:], whole)
    rest = fetch([(whole, teacher), (unit, kept)], sems)
    fold = LOG2E / teacher_temp
    step = 256
    count = step // 128

    def over_columns(c, _):
        at = pl.ds(pl.multiple_of(c * step, step), step)
        weights = whole[:, at]
        acc = jnp.zeros((8, step), f32)
        for r in range(unit.shape[0] // step):
            rows = slice(r * step, (r + 1) * step)
            value = jnp.exp2(dot(unit[rows, :], weights) * fold)
            scores[rows, at] = value.astype(bf16)
            acc = acc + jnp.sum(value.reshape(step // 8, 8, step), axis=0)
        acc = jnp.sum(acc, axis=0, keepdims=True)
        for k in range(count):
            sums[pl.ds(c * count + k, 1), :] = acc[:, k * 128 : (k + 1) * 128]
        return 0

    lax.fori_loop(0, whole.shape[1] // step, over_columns, 0, unroll=4)
    settle(rest)
    columns[...] = jnp.broadcast_to(sums[...][None], columns.shape)


def row_kernel(parts, scores, rows, sums):
    inverse = 1.0 / jnp.sum(parts[...], axis=0)
    group = 4

    def over_rows(i, _):
        for r in range(group):
            at = pl.ds(pl.multiple_of(i * (group * 128) + r * 128, 128), 128)
            acc = jnp.zeros((128, 128), f32)
            for c in range(scores.shape[1] // 128):
                block = scores[at, c * 128 : (c + 1) * 128].astype(f32)
                acc = acc + block * inverse[c : c + 1, :]
            sums[pl.ds(i * group + r, 1), :] = jnp.sum(acc.T, axis=0, keepdims=True)
        return 0

    lax.fori_loop(0, scores.shape[0] // (group * 128), over_rows, 0, unroll=2)
    rows[...] = jnp.broadcast_to(sums[...].astype(rows.dtype)[None], rows.shape)


def column_kernel(parts, scores, columns, weight):
    turned = (1.0 / jnp.sum(parts[...].astype(f32), axis=0)).T
    for r in range(weight.shape[0] // 128):
        weight[r * 128 : (r + 1) * 128, :] = jnp.broadcast_to(turned[:, r : r + 1], (128, 128))
    step = 64
    tiles = scores.shape[1] // 128

    def over_rows(r, acc):
        at = pl.ds(pl.multiple_of(r * step, step), step)
        w = weight[at, :]
        out = []
        for c in range(tiles):
            block = scores[at, c * 128 : (c + 1) * 128].astype(f32) * w
            out.append(acc[c] + jnp.sum(block.reshape(step // 8, 8, 128), axis=0))
        return tuple(out)

    zeros = tuple(jnp.zeros((8, 128), f32) for _ in range(tiles))
    acc = lax.fori_loop(0, scores.shape[0] // step, over_rows, zeros, unroll=8)
    total = jnp.concatenate([jnp.sum(a, axis=0, keepdims=True) for a in acc], axis=0)
    columns[...] = jnp.broadcast_to(total[None], columns.shape)


def last_column_kernel(here, parts, scores, own, *refs):
    blocks, (columns, student, whole, weight, sems) = refs[:-5], refs[-5:]
    hops = (len(blocks) + 1) // 2
    place_blocks(here, own[own.shape[0] // 2 :, :], blocks[:hops], blocks[hops:], whole)
    copies = fetch([(whole, student)], sems)
    column_kernel(parts, scores, columns, weight)
    settle(copies)


def student_kernel(index, hidden, head, unit, teacher, student, *refs):
    masked, scale_out, unit_out, grad, total = refs[:5]
    v_hidden, v_head, v_unit, v_teacher, whole, halves, sems = refs[5:]
    copies = fetch(
        [
            (hidden, v_hidden),
            (head, v_head),
            (unit, v_unit),
            (teacher, v_teacher),
            (student, whole),
        ],
        sems,
    )
    slots, tokens = v_hidden.shape[0], v_unit.shape[0]
    wanted = jnp.broadcast_to(index[...].astype(f32), (128, slots)).T[:, 0:1]
    chosen = wanted == lax.broadcasted_iota(jnp.int32, (slots, tokens), 1).astype(f32)
    chosen = chosen.astype(f32).astype(bf16)
    settle(copies[:2])
    neck = dot(v_hidden[...], v_head[...])
    scale = lax.rsqrt(jnp.sum(neck * neck, axis=1, keepdims=True) + norm_eps)
    unit_float = neck * scale
    width = v_head.shape[1]
    unit_out[:, :width] = unit_float
    unit_out[:, width:] = jnp.broadcast_to(scale, (unit_float.shape[0], 128))
    student = unit_float.astype(bf16)
    settle(copies[2:3])
    picked = dot(chosen, v_unit[...]).astype(bf16)
    settle(copies[3:])
    fold = LOG2E / teacher_temp
    step = 256
    total_acc = jnp.zeros((slots, 1), f32)
    for c in range(whole.shape[1] // step):
        at = slice(c * step, (c + 1) * step)
        masked[:, at] = jnp.exp2(dot(picked, v_teacher[:, at]) * fold)
        weights = whole[:, at]
        wide = weights.astype(f32)
        scale_p = lax.rsqrt(jnp.sum(wide * wide, axis=0, keepdims=True) + norm_eps) / student_temp
        scale_out[:, at] = jnp.broadcast_to(scale_p, (8, step))
        soft = jnp.exp2(dot(student, weights) * (scale_p * LOG2E))
        total_acc = total_acc + jnp.sum(soft, axis=1, keepdims=True)
        halves[:slots, at], halves[slots:, at] = split(soft * scale_p)
    both = dot(halves[...], whole[...], NT)
    grad[...] = both[:slots] + both[slots:]
    total[...] = jnp.broadcast_to(total_acc, total.shape)


def goal_kernel(
    here,
    parts,
    masked,
    unit,
    scale_p,
    whole,
    grad,
    total,
    keep,
    give,
    out,
    v_scale,
    v_whole,
    v_total,
    halves,
    sems,
):
    slots, width = grad.shape
    step = 512
    count = whole.shape[1] // step
    copies = fetch([(scale_p, v_scale), (total, v_total), (grad, out.at[:, :width])], sems)
    weights = fetch([(whole, v_whole)], sems, 3)
    inverse = 1.0 / jnp.sum(parts[...], axis=0)
    goal_acc = jnp.zeros((slots, 128), f32)
    settle(copies[:1])
    for c in range(count):
        pieces = []
        for k in range(c * (step // 128), (c + 1) * (step // 128)):
            at = slice(k * 128, (k + 1) * 128)
            goal = masked[:, at] * inverse[k : k + 1, :]
            goal_acc = goal_acc + goal
            pieces.append(goal * v_scale[0:1, at])
        at = slice(c * step, (c + 1) * step)
        halves[:slots, at], halves[slots:, at] = split(jnp.concatenate(pieces, axis=1))
    settle(weights)
    both = dot(halves[...], v_whole[...], NT)
    grad_acc = both[:slots] + both[slots:]
    out[:, width : 2 * width] = grad_acc
    goal_total = jnp.sum(goal_acc, axis=1, keepdims=True)
    rounded = unit[:, :width].astype(bf16).astype(f32)
    goal_dot = jnp.sum(rounded * grad_acc, axis=1, keepdims=True)
    lane = lax.broadcasted_iota(jnp.int32, (slots, 128), 1)
    settle(copies[1:])
    sums = jnp.where(lane == 0, v_total[...], jnp.where(lane == 1, goal_total, goal_dot)).T
    rows = [sums[k : k + 1, c : c + 128] for k in range(3) for c in range(0, slots, 128)]
    tile = jnp.concatenate(rows + [jnp.zeros((8 - len(rows), 128), f32)], axis=0)
    out[:, 2 * width :] = jnp.broadcast_to(tile[None], (slots // 8, 8, 128)).reshape(slots, 128)
    half = slots // 2
    keep[...] = out[pl.ds(pl.multiple_of(here[1] * half, half), half), :]
    give[...] = out[pl.ds(pl.multiple_of((1 - here[1]) * half, half), half), :]


def add_kernel(first, second, out):
    out[...] = first[...] + second[...]


def slots_kernel(here, counts, parts, unit_float, out, loss):
    count = counts[here[0]]
    share, width = parts.shape[1], unit_float.shape[1] - 128
    mine = jnp.sum(parts[...], axis=0)
    sums = mine[:, 2 * width :]
    slot = 128 * lax.broadcasted_iota(jnp.int32, (2, 128), 0)
    slot = slot + lax.broadcasted_iota(jnp.int32, (2, 128), 1)
    live = jnp.where(slot < count, 1.0, 0.0)
    loss[...] = live * (jnp.log(sums[0:2, :]) - sums[4:6, :] / sums[2:4, :])
    at = here[1] * (unit_float.shape[0] // 2) + lax.div(here[2], 2) * share
    at = pl.multiple_of(at, share)
    row = lax.div(at, 128)
    pick = lax.broadcasted_iota(jnp.int32, (share, 128), 1) == (
        lax.rem(at, 128) + lax.broadcasted_iota(jnp.int32, (share, 128), 0)
    )

    def column(first, second):
        line = jnp.where(row == 0, first, second)
        return jnp.sum(jnp.where(pick, line, 0.0), axis=1, keepdims=True)

    soft_total = column(sums[0:1, :], sums[1:2, :])
    goal_total = column(sums[2:3, :], sums[3:4, :])
    unit = unit_float[pl.ds(at, share), :width]
    scale = unit_float[pl.ds(at, share), width : width + 1]
    soft, goal = mine[:, :width] / soft_total, mine[:, width : 2 * width] / goal_total
    slot = at + lax.broadcasted_iota(jnp.int32, (share, 1), 0)
    unit_grad = jnp.where(slot < count, soft - goal, 0.0)
    inner = jnp.sum(unit * unit_grad, axis=1, keepdims=True)
    neck_grad = scale * (unit_grad - unit * inner)
    halves = jnp.concatenate([neck_grad[:, : width // 2], neck_grad[:, width // 2 :]], axis=0)
    out[...] = jnp.broadcast_to(halves.astype(bf16)[None], out.shape)


def hidden_kernel(parts, head, hidden):
    count, double, half = parts.shape
    share = double // 2
    wide = parts[...].astype(f32).reshape(count // 2, 2, double, half)
    halves = []
    for k in range(2):
        rows = [wide[:, c, k * share : (k + 1) * share, :] for c in range(2)]
        rows = [part.reshape(count // 2 * share, half) for part in rows]
        halves.append(jnp.concatenate(rows, axis=0))
    neck_grad = jnp.concatenate(halves, axis=1).astype(bf16)
    step = 512
    for c in range(head.shape[0] // step):
        at = slice(c * step, (c + 1) * step)
        hidden[:, at] = dot(neck_grad, head[at, :], NT).astype(bf16)


def exchange(blocks, axis, groups=None):
    return lax.all_to_all(blocks, axis, 0, 0, tiled=True, axis_index_groups=groups)


def shards(
    teacher_hidden,
    head_teacher,
    proto_teacher,
    student_hidden,
    head_student,
    proto_student,
    mask_index,
    mask_count,
):
    toks, protos = lax.axis_size("tok"), lax.axis_size("proto")
    tok, proto = lax.axis_index("tok"), lax.axis_index("proto")
    tok_dev, slots = teacher_hidden.shape[0], student_hidden.shape[0]
    depth = teacher_hidden.shape[1]
    width, local = head_teacher.shape[1], proto_teacher.shape[1]
    lines = local // 128
    share = slots // protos
    here = jnp.stack([tok, proto % 2, proto])
    dma = pltpu.SemaphoreType.DMA

    swap = [(i, i ^ 1) for i in range(protos)]
    along = []
    for t in range(toks):
        for p in range(protos):
            to = (t + (1 if p % 2 == 0 else -1)) % toks
            along.append((t * protos + p, to * protos + p))
    rows = proto_teacher.shape[0]

    chips = protos // 2
    groups = [[2 * k + c for k in range(chips)] for c in range(2)]
    copies, both = call(
        heads_kernel,
        (pltpu.HBM((chips, depth // protos, 2 * width), bf16), shaped((2 * rows, local), bf16)),
        [HB] * 4,
        (HB, VM),
        (0, MIB),
        [pltpu.VMEM((depth // protos, 2 * width), bf16), dma((4 + chips,))],
    )(far(head_teacher), far(head_student), far(proto_teacher), far(proto_student))
    mine = exchange(copies, "proto", groups)
    sibling = lax.ppermute(both, "proto", swap)
    chains = call(
        join_kernel,
        (shaped((2 * rows, local), bf16),) * 2,
        [VM, VM],
        (VM, VM),
        (0, MIB),
    )(both, sibling)
    teacher_own, student_own = chains
    hops = toks // 2
    hidden = teacher_hidden
    came, crossed = [], []
    for hop in range(hops):
        sent = came[-1] if hop else teacher_own
        came.append(lax.ppermute(sent if hop < hops - 1 else sent[:rows], ("tok", "proto"), along))
        if hop < hops - 1:
            crossed.append(lax.ppermute(came[-1][rows:], "proto", swap))
        if hop == 1:
            hidden, mine, _ = lax.optimization_barrier((hidden, mine, came[-1]))
            other = lax.ppermute(mine, "proto", swap)
        if hop == hops - 2:
            student_own, _ = lax.optimization_barrier((student_own, came[-1]))
    late, late_crossed = [lax.ppermute(student_own, ("tok", "proto"), along)], []
    staged = call(
        stage_kernel,
        pltpu.VMEM(hidden.shape, bf16),
        [HB],
        VM,
        (0, 16 * MIB),
        [dma((4,))],
    )(far(hidden))
    unit_teacher, full_head = call(
        neck_kernel,
        (
            shaped((tok_dev, width), bf16),
            pltpu.HBM((chips, depth // chips, width), bf16),
        ),
        [SM, VM, VM, VM],
        (VM, HB),
        (2 * tok_dev * depth * width, 10 * MIB),
        [pltpu.VMEM((depth, width), bf16), dma((2,))],
    )(here, held(staged), mine, other)
    full_head = full_head.reshape(depth, width)

    blocks = came + crossed
    scores, whole_teacher, unit_kept, columns = call(
        scores_kernel,
        (
            pltpu.VMEM((tok_dev, local), bf16),
            pltpu.HBM((toks * rows, local), bf16),
            pltpu.HBM((tok_dev, width), bf16),
            shaped((toks, lines, 128), f32),
        ),
        [SM] + [VM] * (2 + len(blocks)),
        (VM, HB, HB, VM),
        (2 * tok_dev * local * width, 12 * MIB),
        [
            pltpu.VMEM((toks * rows, local), bf16),
            pltpu.VMEM((lines, 128), f32),
            dma((2,)),
        ],
    )(here, unit_teacher, both, *blocks)

    row_call = call(
        row_kernel,
        shaped((protos, tok_dev // 128, 128), bf16),
        [VM, VM],
        VM,
        (2 * tok_dev * local, 8 * MIB),
        [pltpu.VMEM((tok_dev // 128, 128), f32)],
    )
    column_call = call(
        column_kernel,
        shaped((toks, lines, 128), f32),
        [VM, VM],
        VM,
        (2 * tok_dev * local, 8 * MIB),
        [pltpu.VMEM((tok_dev, 128), f32)],
    )
    last_column_call = call(
        last_column_kernel,
        (shaped((toks, lines, 128), f32), pltpu.HBM((toks * rows, local), bf16)),
        [SM] + [VM] * (2 + 2 * hops),
        (VM, HB),
        (2 * tok_dev * local, 8 * MIB),
        [
            pltpu.VMEM((toks * rows, local), bf16),
            pltpu.VMEM((tok_dev, 128), f32),
            dma((1,)),
        ],
    )

    def onward(values):
        values, late[-1], *late_crossed[:] = lax.optimization_barrier(
            (values, late[-1], *late_crossed)
        )
        if len(late) < hops:
            late_crossed.append(lax.ppermute(late[-1][rows:], "proto", swap))
            sent = late[-1] if len(late) < hops - 1 else late[-1][:rows]
            late.append(lax.ppermute(sent, ("tok", "proto"), along))
        return values

    columns = onward(columns)
    sums = row_call(exchange(columns, "tok"), held(scores))
    sums = onward(sums)
    columns = column_call(exchange(sums, "proto"), held(scores))
    columns = onward(columns)
    sums = row_call(exchange(columns, "tok"), held(scores))
    sums = onward(sums)
    columns, whole_student = last_column_call(
        here, exchange(sums, "proto"), held(scores), both, *late, *late_crossed
    )
    columns, whole_student = lax.optimization_barrier((columns, whole_student))

    rows = toks * rows
    masked, scale_p, unit_float, grad, soft_total = call(
        student_kernel,
        (
            pltpu.VMEM((slots, local), f32),
            pltpu.HBM((8, local), f32),
            pltpu.VMEM((slots, width + 128), f32),
            pltpu.HBM((slots, width), f32),
            pltpu.HBM((slots, 128), f32),
        ),
        [VM] + [HB] * 5,
        (VM,) * 5,
        (10 * slots * local * width, 8 * MIB),
        [
            pltpu.VMEM((slots, depth), bf16),
            pltpu.VMEM((depth, width), bf16),
            pltpu.VMEM((tok_dev, width), bf16),
            pltpu.VMEM((rows, local), bf16),
            pltpu.VMEM((rows, local), bf16),
            pltpu.VMEM((2 * slots, local), bf16),
            dma((5,)),
        ],
    )(
        mask_index.reshape(1, slots),
        far(student_hidden),
        far(full_head),
        far(unit_kept),
        far(whole_teacher),
        far(whole_student),
    )

    lanes = 2 * width + 128
    keep, give = call(
        goal_kernel,
        (shaped((slots // 2, lanes), f32),) * 2,
        [SM] + [VM] * 3 + [HB] * 4,
        (VM, VM),
        (4 * slots * local * width, 4 * MIB),
        [
            pltpu.VMEM((slots, lanes), f32),
            pltpu.VMEM((8, local), f32),
            pltpu.VMEM((rows, local), bf16),
            pltpu.VMEM((slots, 128), f32),
            pltpu.VMEM((2 * slots, local), bf16),
            dma((4,)),
        ],
    )(
        here,
        exchange(columns, "tok"),
        held(masked),
        held(unit_float),
        far(scale_p),
        far(whole_student),
        far(grad),
        far(soft_total),
    )
    parts = call(add_kernel, shaped((slots // 2, lanes), f32), [VM, VM], VM, (0, MIB))(
        keep, lax.ppermute(give, "proto", swap)
    )
    parts = exchange(parts.reshape(chips, share, lanes), "proto", groups)
    finals, row_loss = call(
        slots_kernel,
        (shaped((protos, 2 * share, width // 2), bf16), shaped((slots // 128, 128), f32)),
        [SM, SM, VM, VM],
        (VM, VM),
        (2 * slots * width, MIB),
    )(here, mask_count, parts, held(unit_float))
    hidden_grad = call(
        hidden_kernel,
        shaped(student_hidden.shape, bf16),
        [VM, VM],
        VM,
        (2 * slots * width * depth, 3 * MIB),
    )(exchange(finals, "proto"), full_head)
    return (row_loss.reshape(slots), hidden_grad)


def solution(mesh):
    placed = (
        P("tok", None),
        P("proto", None),
        P("tok", "proto"),
        P("tok", None),
        P("proto", None),
        P("tok", "proto"),
        P("tok"),
        P(),
    )
    return jax.shard_map(
        shards, mesh=mesh, in_specs=placed, out_specs=(P("tok"), P("tok", None)), check_vma=False
    )
```

```python
import jax
import jax.numpy as jnp
from jax import lax
from jax.experimental import pallas as pl
from jax.experimental.pallas import tpu as pltpu
from jax.sharding import PartitionSpec as P

teacher_temp = 0.07
student_temp = 0.1
norm_eps = 1e-06
LOG2E = 1.4426950408889634
MIB = 1024 * 1024
f32 = jnp.float32
bf16 = jnp.bfloat16
VM = pl.BlockSpec(memory_space=pltpu.VMEM)
SM = pl.BlockSpec(memory_space=pltpu.SMEM)
HB = pl.BlockSpec(memory_space=pltpu.HBM)
ANY = pl.BlockSpec(memory_space=pl.ANY)
NT = (((1,), (1,)), ((), ()))


def shaped(shape, dtype):
    return jax.ShapeDtypeStruct(shape, dtype)


def call(kernel, out_shape, in_specs, out_specs, cost, scratch=(), mib=40):
    return pl.pallas_call(
        kernel,
        out_shape=out_shape,
        in_specs=in_specs,
        out_specs=out_specs,
        scratch_shapes=list(scratch),
        cost_estimate=pl.CostEstimate(flops=cost[0], bytes_accessed=cost[1], transcendentals=0),
        compiler_params=pltpu.CompilerParams(vmem_limit_bytes=mib * MIB),
    )


def held(values):
    return pltpu.with_memory_space_constraint(values, pltpu.VMEM)


def far(values):
    return pltpu.with_memory_space_constraint(values, pltpu.HBM)


def dot(left, right, dims=(((1,), (0,)), ((), ()))):
    return lax.dot_general(left, right, dims, preferred_element_type=f32)


def split(values):
    high = values.astype(bf16)
    return high, (values - high.astype(f32)).astype(bf16)


def fetch(pairs, sems, first=0):
    copies = [
        pltpu.make_async_copy(source, target, sems.at[first + k])
        for k, (source, target) in enumerate(pairs)
    ]
    for copy in copies:
        copy.start()
    return copies


def settle(copies):
    for copy in copies:
        copy.wait()


def heads_kernel(teacher, student, first, second, copies, both, v_heads, sems):
    rows, width = first.shape[0], teacher.shape[1]
    heads = fetch([(teacher, v_heads.at[:, :width]), (student, v_heads.at[:, width:])], sems)
    rest = fetch(
        [(first, both.at[pl.ds(0, rows), :]), (second, both.at[pl.ds(rows, rows), :])], sems, 2
    )
    settle(heads)
    rest += fetch([(v_heads, copies.at[k]) for k in range(copies.shape[0])], sems, 4)
    settle(rest)


def stage_kernel(hidden, staged, sems):
    step = hidden.shape[0] // 4
    rows = [pl.ds(k * step, step) for k in range(4)]
    settle(fetch([(hidden.at[at, :], staged.at[at, :]) for at in rows], sems))


def neck_kernel(here, hidden, mine, other, unit, student, head, sems):
    chips, rows, double = mine.shape
    width = double // 2
    near, away = here[1] * rows, (1 - here[1]) * rows
    near, away = (pl.multiple_of(at, rows) for at in (near, away))
    copies = fetch(
        [
            (mine.at[:, :, width:], student.at[:, pl.ds(near, rows), :]),
            (other.at[:, :, width:], student.at[:, pl.ds(away, rows), :]),
        ],
        sems,
    )
    for chip in range(chips):
        at = 2 * rows * chip
        head[pl.ds(pl.multiple_of(at + near, rows), rows), :] = mine[chip, :, :width]
        head[pl.ds(pl.multiple_of(at + away, rows), rows), :] = other[chip, :, :width]
    step = 256
    for k in range(hidden.shape[0] // step):
        at = slice(k * step, (k + 1) * step)
        neck = dot(hidden[at, :], head[...])
        scale = lax.rsqrt(jnp.sum(neck * neck, axis=1, keepdims=True) + norm_eps)
        unit[at, :] = (neck * scale).astype(bf16)
    settle(copies)


def join_kernel(mine, other, teacher, student):
    rows = mine.shape[0] // 2
    teacher[:rows, :] = mine[:rows, :]
    teacher[rows:, :] = other[:rows, :]
    student[:rows, :] = mine[rows:, :]
    student[rows:, :] = other[rows:, :]


def place_blocks(here, own, came, crossed, whole):
    rows = own.shape[0]
    count = whole.shape[0] // rows
    way = 1 - 2 * here[1]

    def put(steps, block):
        origin = lax.rem(here[0] + way * steps + count, count) * rows
        whole[pl.ds(pl.multiple_of(origin, rows), rows), :] = block[:rows, :]

    put(0, own)
    for k, block in enumerate(came):
        put(-(k + 1), block)
    for k, block in enumerate(crossed):
        put(k + 1, block)


def scores_kernel(here, unit, own, *refs):
    blocks, refs = refs[:-7], refs[-7:]
    scores, teacher, kept, columns, whole, sums, sems = refs
    hops = (len(blocks) + 1) // 2
    place_blocks(here, own[: own.shape[0] // 2, :], blocks[:hops], blocks[hops:], whole)
    rest = fetch([(whole, teacher), (unit, kept)], sems)
    fold = LOG2E / teacher_temp
    step = 256
    count = step // 128

    def over_columns(c, _):
        at = pl.ds(pl.multiple_of(c * step, step), step)
        weights = whole[:, at]
        acc = jnp.zeros((8, step), f32)
        for r in range(unit.shape[0] // step):
            rows = slice(r * step, (r + 1) * step)
            value = jnp.exp2(dot(unit[rows, :], weights) * fold)
            scores[rows, at] = value.astype(bf16)
            acc = acc + jnp.sum(value.reshape(step // 8, 8, step), axis=0)
        acc = jnp.sum(acc, axis=0, keepdims=True)
        for k in range(count):
            sums[pl.ds(c * count + k, 1), :] = acc[:, k * 128 : (k + 1) * 128]
        return 0

    lax.fori_loop(0, whole.shape[1] // step, over_columns, 0, unroll=True)
    settle(rest)
    columns[...] = jnp.broadcast_to(sums[...][None], columns.shape)


def row_kernel(parts, scores, rows, sums):
    inverse = 1.0 / jnp.sum(parts[...], axis=0)
    group = 4

    def over_rows(i, _):
        for r in range(group):
            at = pl.ds(pl.multiple_of(i * (group * 128) + r * 128, 128), 128)
            acc = jnp.zeros((128, 128), f32)
            for c in range(scores.shape[1] // 128):
                block = scores[at, c * 128 : (c + 1) * 128].astype(f32)
                acc = acc + block * inverse[c : c + 1, :]
            sums[pl.ds(i * group + r, 1), :] = jnp.sum(acc.T, axis=0, keepdims=True)
        return 0

    lax.fori_loop(0, scores.shape[0] // (group * 128), over_rows, 0, unroll=True)
    rows[...] = jnp.broadcast_to(sums[...].astype(rows.dtype)[None], rows.shape)


def column_kernel(parts, scores, columns, weight):
    turned = (1.0 / jnp.sum(parts[...].astype(f32), axis=0)).T
    for r in range(weight.shape[0] // 128):
        weight[r * 128 : (r + 1) * 128, :] = jnp.broadcast_to(turned[:, r : r + 1], (128, 128))
    step = 64
    tiles = scores.shape[1] // 128

    def over_rows(r, acc):
        at = pl.ds(pl.multiple_of(r * step, step), step)
        w = weight[at, :]
        out = []
        for c in range(tiles):
            block = scores[at, c * 128 : (c + 1) * 128].astype(f32) * w
            out.append(acc[c] + jnp.sum(block.reshape(step // 8, 8, 128), axis=0))
        return tuple(out)

    zeros = tuple(jnp.zeros((8, 128), f32) for _ in range(tiles))
    acc = lax.fori_loop(0, scores.shape[0] // step, over_rows, zeros, unroll=8)
    total = jnp.concatenate([jnp.sum(a, axis=0, keepdims=True) for a in acc], axis=0)
    columns[...] = jnp.broadcast_to(total[None], columns.shape)


def last_column_kernel(here, parts, scores, own, *refs):
    blocks, (columns, student, whole, weight, sems) = refs[:-5], refs[-5:]
    hops = (len(blocks) + 1) // 2
    place_blocks(here, own[own.shape[0] // 2 :, :], blocks[:hops], blocks[hops:], whole)
    copies = fetch([(whole, student)], sems)
    column_kernel(parts, scores, columns, weight)
    settle(copies)


def student_kernel(index, hidden, head, unit, teacher, student, *refs):
    masked, scale_out, unit_out, grad, total = refs[:5]
    v_hidden, v_head, v_unit, v_teacher, whole, halves, sems = refs[5:]
    copies = fetch(
        [
            (hidden, v_hidden),
            (head, v_head),
            (unit, v_unit),
            (teacher, v_teacher),
            (student, whole),
        ],
        sems,
    )
    slots, tokens = v_hidden.shape[0], v_unit.shape[0]
    wanted = jnp.broadcast_to(index[...].astype(f32), (128, slots)).T[:, 0:1]
    chosen = wanted == lax.broadcasted_iota(jnp.int32, (slots, tokens), 1).astype(f32)
    chosen = chosen.astype(f32).astype(bf16)
    settle(copies[:2])
    neck = dot(v_hidden[...], v_head[...])
    scale = lax.rsqrt(jnp.sum(neck * neck, axis=1, keepdims=True) + norm_eps)
    unit_float = neck * scale
    width = v_head.shape[1]
    unit_out[:, :width] = unit_float
    unit_out[:, width:] = jnp.broadcast_to(scale, (unit_float.shape[0], 128))
    student = unit_float.astype(bf16)
    settle(copies[2:3])
    picked = dot(chosen, v_unit[...]).astype(bf16)
    settle(copies[3:])
    fold = LOG2E / teacher_temp
    step = 256
    total_acc = jnp.zeros((slots, 1), f32)
    for c in range(whole.shape[1] // step):
        at = slice(c * step, (c + 1) * step)
        masked[:, at] = jnp.exp2(dot(picked, v_teacher[:, at]) * fold)
        weights = whole[:, at]
        wide = weights.astype(f32)
        scale_p = lax.rsqrt(jnp.sum(wide * wide, axis=0, keepdims=True) + norm_eps) / student_temp
        scale_out[:, at] = jnp.broadcast_to(scale_p, (8, step))
        soft = jnp.exp2(dot(student, weights) * (scale_p * LOG2E))
        total_acc = total_acc + jnp.sum(soft, axis=1, keepdims=True)
        halves[:slots, at], halves[slots:, at] = split(soft * scale_p)
    both = dot(halves[...], whole[...], NT)
    grad[...] = both[:slots] + both[slots:]
    total[...] = jnp.broadcast_to(total_acc, total.shape)


def goal_kernel(
    here,
    parts,
    masked,
    unit,
    scale_p,
    whole,
    grad,
    total,
    keep,
    give,
    out,
    v_scale,
    v_whole,
    v_total,
    halves,
    sems,
):
    slots, width = grad.shape
    step = 512
    count = whole.shape[1] // step
    copies = fetch([(scale_p, v_scale), (total, v_total), (grad, out.at[:, :width])], sems)
    weights = fetch([(whole, v_whole)], sems, 3)
    inverse = 1.0 / jnp.sum(parts[...], axis=0)
    goal_acc = jnp.zeros((slots, 128), f32)
    settle(copies[:1])
    for c in range(count):
        pieces = []
        for k in range(c * (step // 128), (c + 1) * (step // 128)):
            at = slice(k * 128, (k + 1) * 128)
            goal = masked[:, at] * inverse[k : k + 1, :]
            goal_acc = goal_acc + goal
            pieces.append(goal * v_scale[0:1, at])
        at = slice(c * step, (c + 1) * step)
        halves[:slots, at], halves[slots:, at] = split(jnp.concatenate(pieces, axis=1))
    settle(weights)
    both = dot(halves[...], v_whole[...], NT)
    grad_acc = both[:slots] + both[slots:]
    out[:, width : 2 * width] = grad_acc
    goal_total = jnp.sum(goal_acc, axis=1, keepdims=True)
    rounded = unit[:, :width].astype(bf16).astype(f32)
    goal_dot = jnp.sum(rounded * grad_acc, axis=1, keepdims=True)
    lane = lax.broadcasted_iota(jnp.int32, (slots, 128), 1)
    settle(copies[1:])
    sums = jnp.where(lane == 0, v_total[...], jnp.where(lane == 1, goal_total, goal_dot)).T
    rows = [sums[k : k + 1, c : c + 128] for k in range(3) for c in range(0, slots, 128)]
    tile = jnp.concatenate(rows + [jnp.zeros((8 - len(rows), 128), f32)], axis=0)
    out[:, 2 * width :] = jnp.broadcast_to(tile[None], (slots // 8, 8, 128)).reshape(slots, 128)
    half = slots // 2
    keep[...] = out[pl.ds(pl.multiple_of(here[1] * half, half), half), :]
    give[...] = out[pl.ds(pl.multiple_of((1 - here[1]) * half, half), half), :]


def add_kernel(first, second, out):
    out[...] = first[...] + second[...]


def slots_kernel(here, counts, parts, unit_float, out, loss):
    count = counts[here[0]]
    share, width = parts.shape[1], unit_float.shape[1] - 128
    mine = jnp.sum(parts[...], axis=0)
    sums = mine[:, 2 * width :]
    slot = 128 * lax.broadcasted_iota(jnp.int32, (2, 128), 0)
    slot = slot + lax.broadcasted_iota(jnp.int32, (2, 128), 1)
    live = jnp.where(slot < count, 1.0, 0.0)
    loss[...] = live * (jnp.log(sums[0:2, :]) - sums[4:6, :] / sums[2:4, :])
    at = here[1] * (unit_float.shape[0] // 2) + lax.div(here[2], 2) * share
    at = pl.multiple_of(at, share)
    row = lax.div(at, 128)
    pick = lax.broadcasted_iota(jnp.int32, (share, 128), 1) == (
        lax.rem(at, 128) + lax.broadcasted_iota(jnp.int32, (share, 128), 0)
    )

    def column(first, second):
        line = jnp.where(row == 0, first, second)
        return jnp.sum(jnp.where(pick, line, 0.0), axis=1, keepdims=True)

    soft_total = column(sums[0:1, :], sums[1:2, :])
    goal_total = column(sums[2:3, :], sums[3:4, :])
    unit = unit_float[pl.ds(at, share), :width]
    scale = unit_float[pl.ds(at, share), width : width + 1]
    soft, goal = mine[:, :width] / soft_total, mine[:, width : 2 * width] / goal_total
    slot = at + lax.broadcasted_iota(jnp.int32, (share, 1), 0)
    unit_grad = jnp.where(slot < count, soft - goal, 0.0)
    inner = jnp.sum(unit * unit_grad, axis=1, keepdims=True)
    neck_grad = scale * (unit_grad - unit * inner)
    halves = jnp.concatenate([neck_grad[:, : width // 2], neck_grad[:, width // 2 :]], axis=0)
    out[...] = jnp.broadcast_to(halves.astype(bf16)[None], out.shape)


def hidden_kernel(parts, head, hidden):
    count, double, half = parts.shape
    share = double // 2
    wide = parts[...].astype(f32).reshape(count // 2, 2, double, half)
    halves = []
    for k in range(2):
        rows = [wide[:, c, k * share : (k + 1) * share, :] for c in range(2)]
        rows = [part.reshape(count // 2 * share, half) for part in rows]
        halves.append(jnp.concatenate(rows, axis=0))
    neck_grad = jnp.concatenate(halves, axis=1).astype(bf16)
    step = 512
    for c in range(head.shape[0] // step):
        at = slice(c * step, (c + 1) * step)
        hidden[:, at] = dot(neck_grad, head[at, :], NT).astype(bf16)


def exchange(blocks, axis, groups=None):
    return lax.all_to_all(blocks, axis, 0, 0, tiled=True, axis_index_groups=groups)


def shards(
    teacher_hidden,
    head_teacher,
    proto_teacher,
    student_hidden,
    head_student,
    proto_student,
    mask_index,
    mask_count,
):
    toks, protos = lax.axis_size("tok"), lax.axis_size("proto")
    tok, proto = lax.axis_index("tok"), lax.axis_index("proto")
    tok_dev, slots = teacher_hidden.shape[0], student_hidden.shape[0]
    depth = teacher_hidden.shape[1]
    width, local = head_teacher.shape[1], proto_teacher.shape[1]
    lines = local // 128
    share = slots // protos
    here = jnp.stack([tok, proto % 2, proto])
    dma = pltpu.SemaphoreType.DMA

    swap = [(i, i ^ 1) for i in range(protos)]
    along = []
    for t in range(toks):
        for p in range(protos):
            to = (t + (1 if p % 2 == 0 else -1)) % toks
            along.append((t * protos + p, to * protos + p))
    rows = proto_teacher.shape[0]

    chips = protos // 2
    groups = [[2 * k + c for k in range(chips)] for c in range(2)]
    copies, both = call(
        heads_kernel,
        (pltpu.HBM((chips, depth // protos, 2 * width), bf16), shaped((2 * rows, local), bf16)),
        [HB] * 4,
        (HB, VM),
        (0, MIB),
        [pltpu.VMEM((depth // protos, 2 * width), bf16), dma((4 + chips,))],
    )(far(head_teacher), far(head_student), far(proto_teacher), far(proto_student))
    mine = exchange(copies, "proto", groups)
    sibling = lax.ppermute(both, "proto", swap)
    chains = call(
        join_kernel,
        (shaped((2 * rows, local), bf16),) * 2,
        [VM, VM],
        (VM, VM),
        (0, MIB),
    )(both, sibling)
    teacher_own, student_own = chains
    hops = toks // 2
    hidden = teacher_hidden
    came, crossed = [], []
    for hop in range(hops):
        sent = came[-1] if hop else teacher_own
        came.append(lax.ppermute(sent if hop < hops - 1 else sent[:rows], ("tok", "proto"), along))
        if hop < hops - 1:
            crossed.append(lax.ppermute(came[-1][rows:], "proto", swap))
        if hop == 1:
            hidden, mine, _ = lax.optimization_barrier((hidden, mine, came[-1]))
            other = lax.ppermute(mine, "proto", swap)
        if hop == hops - 2:
            student_own, _ = lax.optimization_barrier((student_own, came[-1]))
    late, late_crossed = [lax.ppermute(student_own, ("tok", "proto"), along)], []
    staged = call(
        stage_kernel,
        pltpu.VMEM(hidden.shape, bf16),
        [HB],
        VM,
        (0, 16 * MIB),
        [dma((4,))],
    )(far(hidden))
    unit_teacher, full_head = call(
        neck_kernel,
        (
            shaped((tok_dev, width), bf16),
            pltpu.HBM((chips, depth // chips, width), bf16),
        ),
        [SM, VM, VM, VM],
        (VM, HB),
        (2 * tok_dev * depth * width, 10 * MIB),
        [pltpu.VMEM((depth, width), bf16), dma((2,))],
    )(here, held(staged), mine, other)
    full_head = full_head.reshape(depth, width)

    blocks = came + crossed
    scores, whole_teacher, unit_kept, columns = call(
        scores_kernel,
        (
            pltpu.VMEM((tok_dev, local), bf16),
            pltpu.HBM((toks * rows, local), bf16),
            pltpu.HBM((tok_dev, width), bf16),
            shaped((toks, lines, 128), f32),
        ),
        [SM] + [VM] * (2 + len(blocks)),
        (VM, HB, HB, VM),
        (2 * tok_dev * local * width, 12 * MIB),
        [
            pltpu.VMEM((toks * rows, local), bf16),
            pltpu.VMEM((lines, 128), f32),
            dma((2,)),
        ],
    )(here, unit_teacher, both, *blocks)

    row_call = call(
        row_kernel,
        shaped((protos, tok_dev // 128, 128), bf16),
        [VM, VM],
        VM,
        (2 * tok_dev * local, 8 * MIB),
        [pltpu.VMEM((tok_dev // 128, 128), f32)],
    )
    column_call = call(
        column_kernel,
        shaped((toks, lines, 128), f32),
        [VM, VM],
        VM,
        (2 * tok_dev * local, 8 * MIB),
        [pltpu.VMEM((tok_dev, 128), f32)],
    )
    last_column_call = call(
        last_column_kernel,
        (shaped((toks, lines, 128), f32), pltpu.HBM((toks * rows, local), bf16)),
        [SM] + [VM] * (2 + 2 * hops),
        (VM, HB),
        (2 * tok_dev * local, 8 * MIB),
        [
            pltpu.VMEM((toks * rows, local), bf16),
            pltpu.VMEM((tok_dev, 128), f32),
            dma((1,)),
        ],
    )

    def onward(values):
        values, late[-1], *late_crossed[:] = lax.optimization_barrier(
            (values, late[-1], *late_crossed)
        )
        if len(late) < hops:
            late_crossed.append(lax.ppermute(late[-1][rows:], "proto", swap))
            sent = late[-1] if len(late) < hops - 1 else late[-1][:rows]
            late.append(lax.ppermute(sent, ("tok", "proto"), along))
        return values

    columns = onward(columns)
    sums = row_call(exchange(columns, "tok"), held(scores))
    sums = onward(sums)
    columns = column_call(exchange(sums, "proto"), held(scores))
    columns = onward(columns)
    sums = row_call(exchange(columns, "tok"), held(scores))
    sums = onward(sums)
    columns, whole_student = last_column_call(
        here, exchange(sums, "proto"), held(scores), both, *late, *late_crossed
    )
    columns, whole_student = lax.optimization_barrier((columns, whole_student))

    rows = toks * rows
    masked, scale_p, unit_float, grad, soft_total = call(
        student_kernel,
        (
            pltpu.VMEM((slots, local), f32),
            pltpu.HBM((8, local), f32),
            pltpu.VMEM((slots, width + 128), f32),
            pltpu.HBM((slots, width), f32),
            pltpu.HBM((slots, 128), f32),
        ),
        [VM] + [HB] * 5,
        (VM,) * 5,
        (10 * slots * local * width, 8 * MIB),
        [
            pltpu.VMEM((slots, depth), bf16),
            pltpu.VMEM((depth, width), bf16),
            pltpu.VMEM((tok_dev, width), bf16),
            pltpu.VMEM((rows, local), bf16),
            pltpu.VMEM((rows, local), bf16),
            pltpu.VMEM((2 * slots, local), bf16),
            dma((5,)),
        ],
    )(
        mask_index.reshape(1, slots),
        far(student_hidden),
        far(full_head),
        far(unit_kept),
        far(whole_teacher),
        far(whole_student),
    )

    lanes = 2 * width + 128
    keep, give = call(
        goal_kernel,
        (shaped((slots // 2, lanes), f32),) * 2,
        [SM] + [VM] * 3 + [HB] * 4,
        (VM, VM),
        (4 * slots * local * width, 4 * MIB),
        [
            pltpu.VMEM((slots, lanes), f32),
            pltpu.VMEM((8, local), f32),
            pltpu.VMEM((rows, local), bf16),
            pltpu.VMEM((slots, 128), f32),
            pltpu.VMEM((2 * slots, local), bf16),
            dma((4,)),
        ],
    )(
        here,
        exchange(columns, "tok"),
        held(masked),
        held(unit_float),
        far(scale_p),
        far(whole_student),
        far(grad),
        far(soft_total),
    )
    parts = call(add_kernel, shaped((slots // 2, lanes), f32), [VM, VM], VM, (0, MIB))(
        keep, lax.ppermute(give, "proto", swap)
    )
    parts = exchange(parts.reshape(chips, share, lanes), "proto", groups)
    finals, row_loss = call(
        slots_kernel,
        (shaped((protos, 2 * share, width // 2), bf16), shaped((slots // 128, 128), f32)),
        [SM, SM, VM, VM],
        (VM, VM),
        (2 * slots * width, MIB),
    )(here, mask_count, parts, held(unit_float))
    hidden_grad = call(
        hidden_kernel,
        shaped(student_hidden.shape, bf16),
        [VM, VM],
        VM,
        (2 * slots * width * depth, 3 * MIB),
    )(exchange(finals, "proto"), full_head)
    return (row_loss.reshape(slots), hidden_grad)


def solution(mesh):
    placed = (
        P("tok", None),
        P("proto", None),
        P("tok", "proto"),
        P("tok", None),
        P("proto", None),
        P("tok", "proto"),
        P("tok"),
        P(),
    )
    return jax.shard_map(
        shards, mesh=mesh, in_specs=placed, out_specs=(P("tok"), P("tok", None)), check_vma=False
    )
```
